256 devices in a mesh: dp: 32 (over y, x, z_hi), tensor: 8 (over z_lo, core).
Axes of the slice: x: 4, y: 4, z: 8 (z_hi: 2, z_lo: 4; z = z_hi * 4 + z_lo), core: 2. Of those that a mesh axis runs over, the one named last changes fastest.
Arguments:
- projected: bfloat16 [32, 512, 3, 5120], P('dp', 'tensor'), may hold values from -6 to 6
- projected_tan: bfloat16 [32, 512, 3, 5120], P('dp', 'tensor'), may hold values from -6 to 6
- hidden: bfloat16 [32, 512, 5120], P('dp', 'tensor'), may hold values from -6 to 6
- hidden_tan: bfloat16 [32, 512, 5120], P('dp', 'tensor'), may hold values from -6 to 6
- out_weight: bfloat16 [5120, 5120], P('tensor', 'dp'), may hold values from -0.078125 to 0.078125
- gate_table: float32 [32, 5120], replicated, may hold values from 0.5 to 1.5
- gate_rate: float32 [32, 5120], replicated, may hold values from -6 to 6
- timestep: int32 [32], P('dp'), may hold values from 0 to 31
Outputs:
- block_out: bfloat16 [32, 512, 5120], P('dp', 'tensor')
- block_tan: bfloat16 [32, 512, 5120], P('dp', 'tensor')
The draws below stay inside these ranges and needn't reach their ends.
All inputs are finite; a program needn't handle non-finite values.
Results may differ from the reference program's by a relative error of at most 0.017.
Values may be sent and summed in bfloat16 or wider, within the bound.
A program may use at most 128 MiB of HBM per device.

```python
import math
import jax
import jax.numpy as jnp
from jax import lax

D = 5120
HEADS = 40
HEAD = 128
CLIP_LEN = 512
STEPS = 32
CLIPS = 32
N_TENSOR = 8


def draw_projected(key, part):
    key = jax.random.fold_in(key, 7)
    subkeys = jax.random.split(key, 1)
    shape = (CLIPS, CLIP_LEN, 3, D)
    drawn = jnp.clip(2.0 * jax.random.normal(subkeys[0], shape, jnp.float32), -6.0, 6.0)
    return drawn.astype(jnp.bfloat16)


def plant(result, stream_key, low, largest):
    longest = result.shape.index(max(result.shape))
    spots = []
    for shift in (0, 1):
        where = [jax.random.randint(jax.random.fold_in(stream_key, axis), (), 0, length) for axis, length in enumerate(result.shape)]
        where[longest] = (where[longest] + shift) % result.shape[longest]
        spots.append(tuple(where))
    return result.at[spots[0]].set(low).at[spots[1]].set(largest)


def block_levels(rng, shape, cuts, low, largest):
    gain = 1.0
    for position, blocks in cuts:
        heights = jax.random.uniform(jax.random.fold_in(jax.random.fold_in(rng, 6), position), (blocks,), jnp.float32, low / len(cuts), largest / len(cuts))
        gain = gain * jnp.repeat(jnp.exp(heights), shape[position] // blocks).reshape((-1,) + (1,) * (len(shape) - 1 - position))
    return gain


def noise(stream_key, shape, scale, limit, shards=(), kind=jnp.bfloat16):
    values = scale * jax.random.normal(stream_key, shape, jnp.float32)
    if shards:
        values = values * block_levels(stream_key, shape, shards, -0.22, 0.18)
    return jnp.clip(values, -limit, limit).astype(kind)


def setup_inputs(seed: int = 0) -> dict:
    seeds = jax.random.split(jax.random.key(seed), 9)
    return {
        "projected": draw_projected(jax.random.fold_in(seeds[8], 71), 0),
        "projected_tan": noise(seeds[1], (CLIPS, CLIP_LEN, 3, D), 1.0, 6.0, ((0, 32), (1, 8))),
        "hidden": noise(seeds[2], (CLIPS, CLIP_LEN, D), 1.0, 6.0, ((0, 32), (1, 8))),
        "hidden_tan": noise(seeds[3], (CLIPS, CLIP_LEN, D), 1.0, 6.0, ((0, 32), (1, 8))),
        "out_weight": noise(seeds[4], (D, D), D ** -0.5, 0.078125, ((0, 8), (1, 32))),
        "gate_table": jnp.clip(jax.random.uniform(seeds[5], (STEPS, D), jnp.float32, 0.5, 1.5), 0.5, 1.5),
        "gate_rate": noise(seeds[6], (STEPS, D), 1.0, 6.0, (), jnp.float32),
        "timestep": plant(jax.random.randint(seeds[7], (CLIPS,), 0, STEPS), jax.random.fold_in(seeds[7], 1), 0, STEPS - 1).astype(jnp.int32),
    }


def attend_clip(clip_items):
    packed, packed_tan = clip_items
    length = packed.shape[0]
    shaped = packed.astype(jnp.float32).reshape(length, 3, HEADS, HEAD)
    shaped_tan = packed_tan.astype(jnp.float32).reshape(length, 3, HEADS, HEAD)
    queries, key_rows, value_rows = (shaped[:, 0], shaped[:, 1], shaped[:, 2])
    query_tan, key_tan, value_tan = (shaped_tan[:, 0], shaped_tan[:, 1], shaped_tan[:, 2])
    score_scale = 1.0 / math.sqrt(HEAD)
    scores = jnp.einsum('qhd,khd->hqk', queries, key_rows) * score_scale
    probs = jax.nn.softmax(scores, axis=-1)
    probs_low = probs.astype(jnp.bfloat16).astype(jnp.float32)
    attended = jnp.einsum('hqk,khd->qhd', probs_low, value_rows).astype(jnp.bfloat16)
    scores_tan = (jnp.einsum('qhd,khd->hqk', query_tan, key_rows) + jnp.einsum('qhd,khd->hqk', queries, key_tan)) * score_scale
    probs_tan = probs * (scores_tan - lax.optimization_barrier(jnp.sum(probs * scores_tan, axis=-1, keepdims=True)))
    probs_tan_low = probs_tan.astype(jnp.bfloat16).astype(jnp.float32)
    attended_tan = jnp.einsum('hqk,khd->qhd', probs_tan_low, value_rows) + jnp.einsum('hqk,khd->qhd', probs_low, value_tan)
    return (attended.reshape(length, D), attended_tan.astype(jnp.bfloat16).reshape(length, D))

def project_sum(rows, out_weight):
    group = D // N_TENSOR

    def add_group(total, index):
        start = (index * group).astype(jnp.int32)
        columns = lax.dynamic_slice_in_dim(rows, start, group, 1)
        weight_rows = lax.dynamic_slice_in_dim(out_weight, start, group, 0)
        partial_value = jnp.dot(columns, weight_rows, preferred_element_type=jnp.float32).astype(jnp.bfloat16)
        partial_value = lax.optimization_barrier(partial_value)
        return (total + partial_value.astype(jnp.float32), None)
    start_total = jnp.zeros((rows.shape[0], D), jnp.float32)
    total, unused = lax.scan(add_group, start_total, jnp.arange(N_TENSOR, dtype=jnp.int32))
    return total

def reference(projected, projected_tan, hidden, hidden_tan, out_weight, gate_table, gate_rate, timestep):
    attended, attended_tan = lax.map(attend_clip, (projected, projected_tan))
    projection = project_sum(attended.reshape(-1, D), out_weight).reshape(CLIPS, CLIP_LEN, D)
    projection_tan = project_sum(attended_tan.reshape(-1, D), out_weight).reshape(CLIPS, CLIP_LEN, D)
    gate_rows = gate_table[timestep][:, None, :]
    rate_rows = gate_rate[timestep][:, None, :]
    block_out = (hidden.astype(jnp.float32) + gate_rows * projection).astype(jnp.bfloat16)
    block_tan = (hidden_tan.astype(jnp.float32) + gate_rows * projection_tan + rate_rows * projection).astype(jnp.bfloat16)
    return (block_out, block_tan)
```

```python
import math

import jax
import jax.numpy as jnp
from jax import lax
from jax.experimental import pallas as pl
from jax.experimental.pallas import tpu as pltpu
from jax.sharding import PartitionSpec as P

HEAD = 128
PARTS = 5
LEN = 512
ROWS = 64
NT = 8
SIDE = 4
RING = 8
COLS = 160
SLICE = 1280
TILES = 5
TILE = 256
D = 5120
AHEAD = 2
BLOCK = 256
PEER_ORDER = (6, 4, 7, 5, 2, 3, 1)
SCALE = 1.0 / math.sqrt(HEAD)
MESH = pl.DeviceIdType.MESH
NT_DIMS = (((1,), (1,)), ((), ()))


def place(y, x, z, core):
    return (y * 8 + x * 2 + z // SIDE, (z % SIDE) * 2 + core)


def aligned(value, size, base):
    return pl.ds(pl.multiple_of(value, base), size)


def kernel(
    proj, ptan, hidden, hidden_tan, weight, gate_table, gate_rate, timestep,
    out, out_tan,
    xbuf, att, tok, wbuf, acc, out_send, out_recv, hid, hid_tan, gates, rates,
    fwd_send, fwd_recv, back_send, back_recv, tok_send, tok_recv,
    z_send, z_recv, x_send, x_recv, core_send, core_recv, res_send, res_recv, local_sem, own_sem,
):
    dp, me = lax.axis_index("dp"), lax.axis_index("tensor")
    y, x, z_hi = dp // 8, (dp % 8) // 2, dp % 2
    z_lo, core = me // 2, me % 2
    z = z_hi * SIDE + z_lo
    lane = (core * SIDE + z_lo) * HEAD
    z_right = place(y, x, (z + 1) % RING, core)
    z_left = place(y, x, (z + RING - 1) % RING, core)
    x_peers = [place(y, (x + k) % SIDE, z, core) for k in range(1, SIDE)]
    y_peers = [place((y + k) % SIDE, x, z, core) for k in range(1, SIDE)]
    tensor_peers = [(me + k) % NT for k in range(1, NT)]
    sibling = (dp, z_lo * 2 + 1 - core)

    def remote(src, dst, send, recv, device):
        copy = pltpu.make_async_remote_copy(
            src_ref=src, dst_ref=dst, send_sem=send, recv_sem=recv, device_id=device, device_id_type=MESH
        )
        copy.start()
        return copy

    def wait_bytes(ref, sem):
        pltpu.make_async_copy(ref, ref, sem).wait()

    barrier = pltpu.get_barrier_semaphore()
    greeted = [(dp, peer) for peer in tensor_peers] + [z_right, z_left] + x_peers + y_peers
    for device in greeted:
        pl.semaphore_signal(barrier, inc=1, device_id=device, device_id_type=MESH)
    pl.semaphore_wait(barrier, len(greeted))

    def xor_peer(k):
        result = 0
        for bit in (1, 2, 4):
            mine = (me // bit) % 2
            result = result + bit * ((1 - mine) if k & bit else mine)
        return result

    peers = [xor_peer(k) for k in PEER_ORDER]
    mine_rows = aligned(ROWS * me, ROWS, ROWS)

    def start_forward(j):
        for peer in peers:
            columns = aligned((peer * PARTS + j) * HEAD, HEAD, HEAD)
            for half, source in enumerate((proj, ptan)):
                remote(
                    source.at[:, :, columns],
                    xbuf.at[j, pl.ds(3 * half, 3), mine_rows, :],
                    fwd_send.at[j],
                    fwd_recv.at[j],
                    (dp, peer),
                )
        columns = aligned((me * PARTS + j) * HEAD, HEAD, HEAD)
        for half, source in enumerate((proj, ptan)):
            pltpu.make_async_copy(
                source.at[:, :, columns], xbuf.at[j, pl.ds(3 * half, 3), mine_rows, :], fwd_recv.at[j]
            ).start()

    def start_back(j):
        lanes = aligned(lane, HEAD, HEAD)
        for peer in peers:
            remote(
                att.at[j, :, aligned(ROWS * peer, ROWS, ROWS), :],
                tok.at[j, y, :, :, lanes],
                back_send.at[j],
                back_recv.at[j],
                (dp, peer),
            )
        pltpu.make_async_copy(att.at[j, :, mine_rows, :], tok.at[j, y, :, :, lanes], back_recv.at[j]).start()

    def start_tokens(j):
        wait_bytes(tok.at[j, y], back_recv.at[j])
        for k, peer in enumerate(y_peers):
            remote(tok.at[j, y], tok.at[j, y], tok_send.at[j, k], tok_recv.at[j, k], peer)

    def wait_tokens(j):
        for k in range(SIDE - 1):
            wait_bytes(tok.at[j, (y + SIDE - 1 - k) % SIDE], tok_recv.at[j, k])

    def attend(j):
        def block(b, carry):
            rows = aligned(b * BLOCK, BLOCK, BLOCK)
            q, qt = xbuf[j, 0, rows, :], xbuf[j, 3, rows, :]
            k, v, kt, vt = xbuf[j, 1], xbuf[j, 2], xbuf[j, 4], xbuf[j, 5]
            s = lax.dot_general(q, k, NT_DIMS, preferred_element_type=jnp.float32)
            st = lax.dot_general(
                jnp.concatenate([qt, q], axis=1),
                jnp.concatenate([k, kt], axis=1),
                NT_DIMS,
                preferred_element_type=jnp.float32,
            )
            top = jnp.max(s, axis=-1, keepdims=True)
            e = jnp.exp2((s - top) * (SCALE * math.log2(math.e)))
            probs = e * (1.0 / jnp.sum(e, axis=-1, keepdims=True))
            low = probs.astype(jnp.bfloat16)
            mean = jnp.sum(probs * st, axis=-1, keepdims=True)
            probs_tan = (probs * ((st - mean) * SCALE)).astype(jnp.bfloat16)
            both = jnp.dot(low, jnp.concatenate([v, vt], axis=1), preferred_element_type=jnp.float32)
            tan = jnp.dot(probs_tan, v, preferred_element_type=jnp.float32) + both[:, HEAD:]
            att[j, 0, rows, :] = both[:, :HEAD].astype(jnp.bfloat16)
            att[j, 1, rows, :] = tan.astype(jnp.bfloat16)
            return carry

        lax.fori_loop(0, LEN // BLOCK, block, 0)

    def project(j):
        rows = tok[j].reshape(SIDE * 2 * ROWS, NT * HEAD)

        def tile(n, carry):
            part = lax.dot_general(
                rows,
                wbuf[j, aligned(n * TILE, TILE, TILE), :],
                NT_DIMS,
                preferred_element_type=jnp.float32,
            )
            if j == 0:
                acc[n] = part
            else:
                acc[n] = acc[n] + part
            return carry

        lax.fori_loop(0, TILES, tile, 0)

    def shard(which, parts=pl.ds(0, PARTS)):
        return wbuf.at[
            parts,
            aligned(x * 2 * COLS + (which // SIDE) * COLS, COLS, COLS),
            aligned((core * SIDE + which % SIDE) * HEAD, HEAD, HEAD),
        ]

    def slab(which_x, which_core):
        return wbuf.at[
            :, aligned(which_x * 2 * COLS, 2 * COLS, 2 * COLS), aligned(which_core * SIDE * HEAD, SIDE * HEAD, SIDE * HEAD)
        ]

    locals_ = []
    for j in range(PARTS):
        locals_.append(
            pltpu.make_async_copy(
                weight.at[:, pl.ds(j * HEAD, HEAD)],
                wbuf.at[j, aligned((x * 2 + z_hi) * COLS, COLS, COLS), aligned(lane, HEAD, HEAD)],
                own_sem.at[0],
            )
        )
    for copy in locals_:
        copy.start()
    wait_bytes(shard(z), own_sem.at[0])
    sends = []
    right_parts, left_parts = pl.ds(0, 3), pl.ds(3, 2)

    def ring_step(s):
        to_right, to_left = (z + RING - s) % RING, (z + s) % RING
        if s < 3:
            a, b = shard(to_right), shard(to_left)
        else:
            a, b = shard(to_right, right_parts), shard(to_left, left_parts)
        sends.append(remote(a, a, z_send.at[0, s], z_recv.at[0, s], z_right))
        sends.append(remote(b, b, z_send.at[1, s], z_recv.at[1, s], z_left))

    def ring_wait(s):
        from_left, from_right = (z + RING - s - 1) % RING, (z + s + 1) % RING
        if s < 3:
            a, b = shard(from_left), shard(from_right)
        else:
            a, b = shard(from_left, right_parts), shard(from_right, left_parts)
        wait_bytes(a, z_recv.at[0, s])
        wait_bytes(b, z_recv.at[1, s])

    ring_step(0)
    start_forward(0)
    residual = [
        pltpu.make_async_copy(source, target, local_sem.at[i])
        for i, (source, target) in enumerate(
            ((hidden, hid), (hidden_tan, hid_tan), (gate_table, gates), (gate_rate, rates))
        )
    ]
    for copy in residual:
        copy.start()
    start_forward(1)
    for s in range(1, 4):
        ring_wait(s - 1)
        ring_step(s)
    ring_wait(3)
    own_slab = slab(x, core)
    for k, peer in enumerate(x_peers):
        sends.append(remote(own_slab, own_slab, x_send.at[k], x_recv.at[k], peer))
    sends.append(remote(own_slab, own_slab, core_send.at[0], core_recv.at[0], sibling))

    def relay_slabs():
        for k in range(SIDE - 1):
            piece = slab((x + SIDE - 1 - k) % SIDE, core)
            wait_bytes(piece, x_recv.at[k])
            sends.append(remote(piece, piece, core_send.at[k + 1], core_recv.at[k + 1], sibling))

    def wait_slabs():
        for k in range(SIDE):
            wait_bytes(slab((x + SIDE - k) % SIDE, 1 - core), core_recv.at[k])

    for j in range(PARTS):
        wait_bytes(xbuf.at[j], fwd_recv.at[j])
        if j + AHEAD < PARTS:
            start_forward(j + AHEAD)
        attend(j)
        start_back(j)
        if j >= 1:
            start_tokens(j - 1)
        if j == 3:
            relay_slabs()
    wait_slabs()
    for j in range(3):
        wait_tokens(j)
        project(j)
    start_tokens(4)
    wait_tokens(3)
    project(3)
    wait_tokens(4)
    project(4)

    def send_tile(n):
        total = acc[n].astype(jnp.bfloat16).reshape(SIDE, 2, ROWS, TILE)
        out_send[n] = total
        for k, peer in enumerate(y_peers):
            remote(
                out_send.at[n, (y + k + 1) % SIDE],
                out_recv.at[n, y],
                res_send.at[n, k],
                res_recv.at[n, k],
                peer,
            )
        out_recv[n, y] = out_send[n, y]

    for n in range(TILES):
        send_tile(n)

    for copy in residual:
        copy.wait()
    level = timestep[0]
    levels = lax.broadcasted_iota(jnp.int32, gates.shape, 0)
    gate_row = jnp.sum(jnp.where(levels == level, gates[...], 0.0), axis=0, keepdims=True)
    rate_row = jnp.sum(jnp.where(levels == level, rates[...], 0.0), axis=0, keepdims=True)
    gates[0:1, :] = gate_row
    rates[0:1, :] = rate_row

    for n in range(TILES):
        for k in range(SIDE - 1):
            wait_bytes(out_recv.at[n, (y + SIDE - 1 - k) % SIDE], res_recv.at[n, k])
        for r in range(SIDE):
            columns = pl.ds(r * SLICE + n * TILE, TILE)
            gate, rate = gates[0:1, columns], rates[0:1, columns]
            value = out_recv[n, r, 0].astype(jnp.float32)
            value_tan = out_recv[n, r, 1].astype(jnp.float32)
            out[:, columns] = (hid[:, columns].astype(jnp.float32) + gate * value).astype(jnp.bfloat16)
            out_tan[:, columns] = (
                hid_tan[:, columns].astype(jnp.float32) + gate * value_tan + rate * value
            ).astype(jnp.bfloat16)

    for j in range(PARTS):
        wait_bytes(xbuf.at[j, :, pl.ds(0, LEN - ROWS), :], fwd_send.at[j])
        wait_bytes(att.at[j, :, pl.ds(0, LEN - ROWS), :], back_send.at[j])
        for k in range(SIDE - 1):
            wait_bytes(tok.at[j, y], tok_send.at[j, k])
    for copy in sends:
        copy.wait_send()
    for n in range(TILES):
        for k in range(SIDE - 1):
            wait_bytes(out_send.at[n, 0], res_send.at[n, k])


def shards(projected, projected_tan, hidden, hidden_tan, out_weight, gate_table, gate_rate, timestep):
    proj = jnp.transpose(projected, (0, 2, 1, 3)).reshape(3, ROWS, D)
    ptan = jnp.transpose(projected_tan, (0, 2, 1, 3)).reshape(3, ROWS, D)
    any_spec = pl.BlockSpec(memory_space=pl.ANY)
    vmem = pl.BlockSpec(memory_space=pltpu.VMEM)
    bf16 = jnp.bfloat16
    dma = pltpu.SemaphoreType.DMA
    block_out, block_tan = pl.pallas_call(
        kernel,
        out_shape=(jax.ShapeDtypeStruct((ROWS, D), bf16), jax.ShapeDtypeStruct((ROWS, D), bf16)),
        in_specs=[any_spec] * 7 + [pl.BlockSpec(memory_space=pltpu.SMEM)],
        out_specs=(vmem, vmem),
        scratch_shapes=[
            pltpu.VMEM((PARTS, 6, LEN, HEAD), bf16),
            pltpu.VMEM((PARTS, 2, LEN, HEAD), bf16),
            pltpu.VMEM((PARTS, SIDE, 2, ROWS, NT * HEAD), bf16),
            pltpu.VMEM((PARTS, SLICE, NT * HEAD), bf16),
            pltpu.VMEM((TILES, SIDE * 2 * ROWS, TILE), jnp.float32),
            pltpu.VMEM((TILES, SIDE, 2, ROWS, TILE), bf16),
            pltpu.VMEM((TILES, SIDE, 2, ROWS, TILE), bf16),
            pltpu.VMEM((ROWS, D), bf16),
            pltpu.VMEM((ROWS, D), bf16),
            pltpu.VMEM((32, D), jnp.float32),
            pltpu.VMEM((32, D), jnp.float32),
            dma((PARTS,)),
            dma((PARTS,)),
            dma((PARTS,)),
            dma((PARTS,)),
            dma((PARTS, SIDE - 1)),
            dma((PARTS, SIDE - 1)),
            dma((2, 4)),
            dma((2, 4)),
            dma((SIDE - 1,)),
            dma((SIDE - 1,)),
            dma((SIDE,)),
            dma((SIDE,)),
            dma((TILES, SIDE - 1)),
            dma((TILES, SIDE - 1)),
            dma((4,)),
            dma((1,)),
        ],
        compiler_params=pltpu.CompilerParams(
            collective_id=0, has_side_effects=True, vmem_limit_bytes=56 * 1024 * 1024
        ),
    )(
        proj,
        ptan,
        hidden.reshape(ROWS, D),
        hidden_tan.reshape(ROWS, D),
        out_weight.T,
        gate_table,
        gate_rate,
        timestep,
    )
    return block_out[None], block_tan[None]


def solution(mesh):
    return jax.shard_map(
        shards,
        mesh=mesh,
        in_specs=(
            P("dp", "tensor", None, None),
            P("dp", "tensor", None, None),
            P("dp", "tensor", None),
            P("dp", "tensor", None),
            P("tensor", "dp"),
            P(),
            P(),
            P("dp"),
        ),
        out_specs=(P("dp", "tensor", None), P("dp", "tensor", None)),
        check_vma=False,
    )
```

```python
import math

import jax
import jax.numpy as jnp
from jax import lax
from jax.experimental import pallas as pl
from jax.experimental.pallas import tpu as pltpu
from jax.sharding import PartitionSpec as P

HEAD = 128
PARTS = 5
LEN = 512
ROWS = 64
HALF = 32
NT = 8
SIDE = 4
RING = 8
COLS = 160
SLAB = 320
SLICE = 1280
TILES = 5
TILE = 256
D = 5120
BLOCK = 256
PEER_ORDER = (6, 4, 7, 5, 2, 3, 1)
SCALE = 1.0 / math.sqrt(HEAD)
MESH = pl.DeviceIdType.MESH
NT_DIMS = (((1,), (1,)), ((), ()))


def place(y, x, z, core):
    return (y * 8 + x * 2 + z // SIDE, (z % SIDE) * 2 + core)


def aligned(value, size, base):
    return pl.ds(pl.multiple_of(value, base), size)


def kernel(
    proj, ptan, hidden, hidden_tan, weight, gate_table, gate_rate, timestep,
    out, out_tan,
    xkv, xq, att, tok, wbuf, acc, out_send, out_recv, hid, hid_tan, gates, rates,
    kv_send, kv_recv, q_send, q_recv, back_send, back_recv, tok_send, tok_recv,
    z_send, z_recv, w_send, w_recv, res_send, res_recv, local_sem, own_sem,
):
    dp, me = lax.axis_index("dp"), lax.axis_index("tensor")
    y, x, z_hi = dp // 8, (dp % 8) // 2, dp % 2
    z_lo, core = me // 2, me % 2
    z = z_hi * SIDE + z_lo
    lanes = aligned((core * SIDE + z_lo) * HEAD, HEAD, HEAD)

    def pick(which_core, first, second):
        return first * (1 - which_core) + second * which_core

    rank, own_slot = pick(core, y, x), pick(core, x, y)
    z_right = place(y, x, (z + 1) % RING, core)
    z_left = place(y, x, (z + RING - 1) % RING, core)

    def along_x(k, which_core):
        return place(y, (x + k) % SIDE, z, which_core)

    def along_y(k, which_core):
        return place((y + k) % SIDE, x, z, which_core)

    def row_peer(k):
        return place(pick(core, (y + k) % SIDE, y), pick(core, x, (x + k) % SIDE), z, core)

    def weight_peer(k, which_core):
        return place(pick(which_core, y, (y + k) % SIDE), pick(which_core, (x + k) % SIDE, x), z, which_core)

    def remote(src, dst, send, recv, device):
        copy = pltpu.make_async_remote_copy(
            src_ref=src, dst_ref=dst, send_sem=send, recv_sem=recv, device_id=device, device_id_type=MESH
        )
        copy.start()
        return copy

    def wait_bytes(ref, sem):
        pltpu.make_async_copy(ref, ref, sem).wait()

    barrier = pltpu.get_barrier_semaphore()
    greeted = [(dp, (me + k) % NT) for k in range(1, NT)] + [z_right, z_left]
    for k in range(1, SIDE):
        greeted += [along_x(k, 0), along_x(k, 1), along_y(k, 0), along_y(k, 1)]
    for device in greeted:
        pl.semaphore_signal(barrier, inc=1, device_id=device, device_id_type=MESH)
    own_copies = [
        pltpu.make_async_copy(
            weight.at[:, pl.ds(j * HEAD, HEAD)],
            wbuf.at[j, aligned(own_slot * SLAB + z_hi * COLS, COLS, COLS), lanes],
            own_sem.at[0],
        )
        for j in range(PARTS)
    ]
    for copy in own_copies:
        copy.start()
    residual = [
        pltpu.make_async_copy(source, target, local_sem.at[i])
        for i, (source, target) in enumerate(
            ((hidden, hid), (hidden_tan, hid_tan), (gate_table, gates), (gate_rate, rates))
        )
    ]
    for copy in residual:
        copy.start()
    pl.semaphore_wait(barrier, len(greeted))

    def xor_peer(k):
        result = 0
        for bit in (1, 2, 4):
            mine = (me // bit) % 2
            result = result + bit * ((1 - mine) if k & bit else mine)
        return result

    peers = [xor_peer(k) for k in PEER_ORDER]

    def head_columns(peer, j):
        return aligned((peer * PARTS + j) * HEAD, HEAD, HEAD)

    def start_kv(j):
        for peer in peers:
            for half, source in enumerate((proj, ptan)):
                remote(
                    source.at[pl.ds(1, 2), :, :, head_columns(peer, j)],
                    xkv.at[j, pl.ds(2 * half, 2), me],
                    kv_send.at[j],
                    kv_recv.at[j],
                    (dp, peer),
                )
        for half, source in enumerate((proj, ptan)):
            pltpu.make_async_copy(
                source.at[pl.ds(1, 2), :, :, head_columns(me, j)], xkv.at[j, pl.ds(2 * half, 2), me], kv_recv.at[j]
            ).start()

    def q_index(j, b):
        return j if b is None else j + b

    def start_q(j, b=None):
        blocks = pl.ds(0, 2) if b is None else pl.ds(b, 1)
        i = q_index(j, b)
        for peer in peers:
            for half, source in enumerate((proj, ptan)):
                remote(
                    source.at[0, blocks, :, head_columns(peer, j)],
                    xq.at[j, half, blocks, me],
                    q_send.at[i],
                    q_recv.at[i],
                    (dp, peer),
                )
        for half, source in enumerate((proj, ptan)):
            pltpu.make_async_copy(
                source.at[0, blocks, :, head_columns(me, j)], xq.at[j, half, blocks, me], q_recv.at[i]
            ).start()

    def wait_kv(j):
        wait_bytes(xkv.at[j], kv_recv.at[j])

    def wait_q(j, b=None):
        blocks = pl.ds(0, 2) if b is None else pl.ds(b, 1)
        wait_bytes(xq.at[j, :, blocks], q_recv.at[q_index(j, b)])

    def start_back(j, b=None):
        blocks = pl.ds(0, 2) if b is None else pl.ds(b, 1)
        i = q_index(j, b)
        for peer in peers:
            remote(
                att.at[j, blocks, :, peer],
                tok.at[j, pick(peer % 2, y, x), blocks, :, :, lanes],
                back_send.at[i],
                back_recv.at[i],
                (dp, peer),
            )
        pltpu.make_async_copy(att.at[j, blocks, :, me], tok.at[j, rank, blocks, :, :, lanes], back_recv.at[i]).start()

    def start_tokens(j, b=None):
        blocks = pl.ds(0, 2) if b is None else pl.ds(b, 1)
        i = q_index(j, b)
        mine = tok.at[j, rank, blocks]
        wait_bytes(mine, back_recv.at[i])
        for k in range(1, SIDE):
            remote(mine, mine, tok_send.at[i, k - 1], tok_recv.at[i, k - 1], row_peer(k))

    def wait_tokens(j, b=None):
        blocks = pl.ds(0, 2) if b is None else pl.ds(b, 1)
        for k in range(1, SIDE):
            wait_bytes(tok.at[j, (rank + SIDE - k) % SIDE, blocks], tok_recv.at[q_index(j, b), k - 1])

    def attend(j, b):
        q = xq[j, 0, b].reshape(BLOCK, HEAD)
        qt = xq[j, 1, b].reshape(BLOCK, HEAD)
        k, v, kt, vt = (xkv[j, i].reshape(LEN, HEAD) for i in range(4))
        s = lax.dot_general(q, k, NT_DIMS, preferred_element_type=jnp.float32)
        st = lax.dot_general(
            jnp.concatenate([qt, q], axis=1),
            jnp.concatenate([k, kt], axis=1),
            NT_DIMS,
            preferred_element_type=jnp.float32,
        )
        top = jnp.max(s, axis=-1, keepdims=True)
        e = jnp.exp2((s - top) * (SCALE * math.log2(math.e)))
        probs = e * (1.0 / jnp.sum(e, axis=-1, keepdims=True))
        low = probs.astype(jnp.bfloat16)
        mean = jnp.sum(probs * st, axis=-1, keepdims=True)
        probs_tan = (probs * ((st - mean) * SCALE)).astype(jnp.bfloat16)
        both = jnp.dot(low, jnp.concatenate([v, vt], axis=1), preferred_element_type=jnp.float32)
        tan = jnp.dot(probs_tan, v, preferred_element_type=jnp.float32) + both[:, HEAD:]
        att[j, b, 0] = both[:, :HEAD].astype(jnp.bfloat16).reshape(NT, HALF, HEAD)
        att[j, b, 1] = tan.astype(jnp.bfloat16).reshape(NT, HALF, HEAD)

    def attend_all(j):
        def block(b, carry):
            attend(j, b)
            return carry

        lax.fori_loop(0, 2, block, 0)

    def project(j):
        rows = tok[j].reshape(SIDE * 2 * 2 * HALF, NT * HEAD)

        def tile(n, carry):
            part = lax.dot_general(
                rows,
                wbuf[j, aligned(n * TILE, TILE, TILE), :],
                NT_DIMS,
                preferred_element_type=jnp.float32,
            ).reshape(SIDE, 2, 2 * HALF, TILE)
            if j == 0:
                acc[n] = part
            else:
                acc[n] = acc[n] + part
            return carry

        lax.fori_loop(0, TILES, tile, 0)

    def project_last(j, b):
        rows = tok[j, :, b].reshape(SIDE * 2 * HALF, NT * HEAD)

        def tile(n, carry):
            part = lax.dot_general(
                rows,
                wbuf[j, aligned(n * TILE, TILE, TILE), :],
                NT_DIMS,
                preferred_element_type=jnp.float32,
            ).reshape(SIDE, 2 * HALF, TILE)
            total = (acc[n, :, b] + part).astype(jnp.bfloat16).reshape(SIDE, 2, HALF, TILE)
            out_send[b, :, n] = total
            return carry

        lax.fori_loop(0, TILES, tile, 0)
        for k in range(1, SIDE):
            remote(
                out_send.at[b, (rank + k) % SIDE],
                out_recv.at[b, rank],
                res_send.at[b, k - 1],
                res_recv.at[b, k - 1],
                row_peer(k),
            )
        out_recv[b, rank] = out_send[b, rank]

    def shard(slot, which, parts=pl.ds(0, PARTS)):
        return wbuf.at[
            parts,
            aligned(slot * SLAB + (which // SIDE) * COLS, COLS, COLS),
            aligned((core * SIDE + which % SIDE) * HEAD, HEAD, HEAD),
        ]

    def slab(slot, which_core):
        return wbuf.at[
            :, aligned(slot * SLAB, SLAB, SLAB), aligned(which_core * SIDE * HEAD, SIDE * HEAD, SIDE * HEAD)
        ]

    right_parts, left_parts = pl.ds(0, 3), pl.ds(3, 2)
    ring_sends = []

    def ring_step(s):
        a, b = (z + RING - s) % RING, (z + s) % RING
        if s < 3:
            a, b = shard(own_slot, a), shard(own_slot, b)
        else:
            a, b = shard(own_slot, a, right_parts), shard(own_slot, b, left_parts)
        ring_sends.append(remote(a, a, z_send.at[0, s], z_recv.at[0, s], z_right))
        ring_sends.append(remote(b, b, z_send.at[1, s], z_recv.at[1, s], z_left))

    def fan(which):
        source = shard(own_slot, which)
        for k in range(1, SIDE):
            remote(source, source, w_send.at[k - 1], w_recv.at[k - 1], weight_peer(k, core))
        other = shard(pick(core, y, x), which)
        for k in range(SIDE):
            remote(source, other, w_send.at[3 + k], w_recv.at[3 + k], weight_peer(k, 1 - core))

    def ring_wait(s):
        from_left, from_right = (z + RING - s - 1) % RING, (z + s + 1) % RING
        if s < 3:
            a, b = shard(own_slot, from_left), shard(own_slot, from_right)
        else:
            a, b = shard(own_slot, from_left, right_parts), shard(own_slot, from_right, left_parts)
        wait_bytes(a, z_recv.at[0, s])
        wait_bytes(b, z_recv.at[1, s])
        if s < 3:
            ring_step(s + 1)
            fan(from_left)
            fan(from_right)
        else:
            fan(from_left)

    def wait_weights():
        for k in range(1, SIDE):
            wait_bytes(slab((own_slot + SIDE - k) % SIDE, core), w_recv.at[k - 1])
        for k in range(SIDE):
            wait_bytes(slab((own_slot + SIDE - k) % SIDE, 1 - core), w_recv.at[3 + k])

    wait_bytes(shard(own_slot, z), own_sem.at[0])
    ring_step(0)
    start_kv(0)
    start_q(0)
    fan(z)
    ring_wait(0)
    wait_kv(0)
    start_kv(1)
    ring_wait(1)
    wait_q(0)
    start_q(1)
    attend_all(0)
    start_back(0)
    ring_wait(2)
    wait_kv(1)
    start_kv(2)
    ring_wait(3)
    wait_q(1)
    start_q(2)
    attend_all(1)
    start_back(1)
    start_tokens(0)
    wait_kv(2)
    start_kv(3)
    wait_q(2)
    start_q(3)
    attend_all(2)
    start_back(2)
    start_tokens(1)
    wait_kv(3)
    start_kv(4)
    wait_q(3)
    start_q(4, 0)
    start_q(4, 1)
    attend_all(3)
    start_back(3)
    start_tokens(2)
    wait_weights()
    for j in range(2):
        wait_tokens(j)
        project(j)
    wait_kv(4)
    wait_q(4, 0)
    attend(4, 0)
    start_back(4, 0)
    start_tokens(3)
    wait_q(4, 1)
    attend(4, 1)
    start_back(4, 1)
    wait_tokens(2)
    project(2)
    start_tokens(4, 0)
    wait_tokens(3)
    project(3)
    start_tokens(4, 1)
    wait_tokens(4, 0)
    project_last(4, 0)
    wait_tokens(4, 1)
    project_last(4, 1)

    for copy in residual:
        copy.wait()
    level = timestep[0]
    levels = lax.broadcasted_iota(jnp.int32, gates.shape, 0)
    gate_row = jnp.sum(jnp.where(levels == level, gates[...], 0.0), axis=0, keepdims=True)
    rate_row = jnp.sum(jnp.where(levels == level, rates[...], 0.0), axis=0, keepdims=True)
    gates[0:1, :] = gate_row
    rates[0:1, :] = rate_row

    def finish(b, columns, value, value_tan):
        rows = pl.ds(b * HALF, HALF)
        gate, rate = gates[0:1, columns], rates[0:1, columns]
        out[rows, columns] = (hid[rows, columns].astype(jnp.float32) + gate * value).astype(jnp.bfloat16)
        out_tan[rows, columns] = (
            hid_tan[rows, columns].astype(jnp.float32) + gate * value_tan + rate * value
        ).astype(jnp.bfloat16)

    def finish_straight(b):
        for r in range(SIDE):
            for n in range(TILES):
                value = out_recv[b, r, n].astype(jnp.float32)
                finish(b, pl.ds(r * SLICE + n * TILE, TILE), value[0], value[1])

    def finish_crossed(b):
        lower = lax.broadcasted_iota(jnp.int32, (2 * HALF, HEAD), 1) < HEAD // 2

        def load(r, unit):
            q = unit // 2
            piece = out_recv[b, r, q // 2, :, :, pl.ds((q % 2) * HEAD, HEAD)]
            return piece.astype(jnp.float32).reshape(2 * HALF, HEAD)

        for t in range(D // HEAD):
            found = []
            for g in (2 * t, 2 * t + 1):
                s, rest = g // 20, g % 20
                found.append((rest // 5, 5 * s + rest % 5))
            (r0, u0), (r1, u1) = found
            first = load(r0, u0)
            if u0 % 2:
                first = pltpu.roll(first, HEAD // 2, 1)
            if r0 == r1 and u0 % 2 == 0 and u1 == u0 + 1:
                value = first
            else:
                second = load(r1, u1)
                if u1 % 2 == 0:
                    second = pltpu.roll(second, HEAD // 2, 1)
                value = jnp.where(lower, first, second)
            finish(b, pl.ds(t * HEAD, HEAD), value[:HALF], value[HALF:])

    for b in range(2):
        for k in range(1, SIDE):
            wait_bytes(out_recv.at[b, (rank + SIDE - k) % SIDE], res_recv.at[b, k - 1])
        pl.when(core == 0)(lambda b=b: finish_straight(b))
        pl.when(core == 1)(lambda b=b: finish_crossed(b))

    for j in range(PARTS):
        wait_bytes(xkv.at[j, :, pl.ds(0, NT - 1)], kv_send.at[j])
        for b in (None,) if j < PARTS - 1 else (0, 1):
            blocks = pl.ds(0, 2) if b is None else pl.ds(b, 1)
            i = q_index(j, b)
            wait_bytes(xq.at[j, :, blocks, pl.ds(0, NT - 1)], q_send.at[i])
            wait_bytes(att.at[j, blocks, :, pl.ds(0, NT - 1)], back_send.at[i])
            for k in range(SIDE - 1):
                wait_bytes(tok.at[j, rank, blocks], tok_send.at[i, k])
    for copy in ring_sends:
        copy.wait_send()
    for k in range(7):
        wait_bytes(slab(own_slot, core), w_send.at[k])
    for b in range(2):
        for k in range(SIDE - 1):
            wait_bytes(out_send.at[b, 0], res_send.at[b, k])


def shards(projected, projected_tan, hidden, hidden_tan, out_weight, gate_table, gate_rate, timestep):
    proj = jnp.transpose(projected, (0, 2, 1, 3)).reshape(3, 2, HALF, D)
    ptan = jnp.transpose(projected_tan, (0, 2, 1, 3)).reshape(3, 2, HALF, D)
    any_spec = pl.BlockSpec(memory_space=pl.ANY)
    vmem = pl.BlockSpec(memory_space=pltpu.VMEM)
    bf16 = jnp.bfloat16
    dma = pltpu.SemaphoreType.DMA
    block_out, block_tan = pl.pallas_call(
        kernel,
        out_shape=(jax.ShapeDtypeStruct((ROWS, D), bf16), jax.ShapeDtypeStruct((ROWS, D), bf16)),
        in_specs=[any_spec] * 7 + [pl.BlockSpec(memory_space=pltpu.SMEM)],
        out_specs=(vmem, vmem),
        scratch_shapes=[
            pltpu.VMEM((PARTS, 4, NT, 2, HALF, HEAD), bf16),
            pltpu.VMEM((PARTS, 2, 2, NT, HALF, HEAD), bf16),
            pltpu.VMEM((PARTS, 2, 2, NT, HALF, HEAD), bf16),
            pltpu.VMEM((PARTS, SIDE, 2, 2, HALF, NT * HEAD), bf16),
            pltpu.VMEM((PARTS, SLICE, NT * HEAD), bf16),
            pltpu.VMEM((TILES, SIDE, 2, 2 * HALF, TILE), jnp.float32),
            pltpu.VMEM((2, SIDE, TILES, 2, HALF, TILE), bf16),
            pltpu.VMEM((2, SIDE, TILES, 2, HALF, TILE), bf16),
            pltpu.VMEM((ROWS, D), bf16),
            pltpu.VMEM((ROWS, D), bf16),
            pltpu.VMEM((32, D), jnp.float32),
            pltpu.VMEM((32, D), jnp.float32),
            dma((PARTS,)),
            dma((PARTS,)),
            dma((PARTS + 1,)),
            dma((PARTS + 1,)),
            dma((PARTS + 1,)),
            dma((PARTS + 1,)),
            dma((PARTS + 1, SIDE - 1)),
            dma((PARTS + 1, SIDE - 1)),
            dma((2, 4)),
            dma((2, 4)),
            dma((7,)),
            dma((7,)),
            dma((2, SIDE - 1)),
            dma((2, SIDE - 1)),
            dma((4,)),
            dma((1,)),
        ],
        compiler_params=pltpu.CompilerParams(
            collective_id=0, has_side_effects=True, vmem_limit_bytes=56 * 1024 * 1024
        ),
    )(
        proj,
        ptan,
        hidden.reshape(ROWS, D),
        hidden_tan.reshape(ROWS, D),
        out_weight.T,
        gate_table,
        gate_rate,
        timestep,
    )
    return block_out[None], block_tan[None]


def solution(mesh):
    return jax.shard_map(
        shards,
        mesh=mesh,
        in_specs=(
            P("dp", "tensor", None, None),
            P("dp", "tensor", None, None),
            P("dp", "tensor", None),
            P("dp", "tensor", None),
            P("tensor", "dp"),
            P(),
            P(),
            P("dp"),
        ),
        out_specs=(P("dp", "tensor", None), P("dp", "tensor", None)),
        check_vma=False,
    )
```

```python
import math

import jax
import jax.numpy as jnp
from jax import lax
from jax.experimental import pallas as pl
from jax.experimental.pallas import tpu as pltpu
from jax.sharding import PartitionSpec as P

HEAD = 128
PARTS = 5
LEN = 512
ROWS = 64
BLOCKS = 4
UNIT = ROWS // BLOCKS
ALL = (0, BLOCKS)
GROUPS = ((0, 2), (2, 2))
LAST = 4
NT = 8
SIDE = 4
RING = 8
COLS = 160
SLAB = 320
SLICE = 1280
TILES = 5
TILE = 256
D = 5120
PEER_ORDER = (2, 3, 4, 5, 6, 7, 1)
SCALE = 1.0 / math.sqrt(HEAD)
MESH = pl.DeviceIdType.MESH
NT_DIMS = (((1,), (1,)), ((), ()))


def place(y, x, z, core):
    return (y * 8 + x * 2 + z // SIDE, (z % SIDE) * 2 + core)


def aligned(value, size, base):
    return pl.ds(pl.multiple_of(value, base), size)


def kernel(
    proj, ptan, hidden, hidden_tan, weight, gate_table, gate_rate, timestep,
    out, out_tan,
    xkv, xq, att, tok, wbuf, acc, out_send, out_recv, hid, hid_tan, gates, rates,
    kv_send, kv_recv, q_send, q_recv, back_send, back_recv, tok_send, tok_recv,
    z_send, z_recv, w_send, w_recv, res_send, res_recv, local_sem, own_sem,
):
    dp, me = lax.axis_index("dp"), lax.axis_index("tensor")
    y, x, z_hi = dp // 8, (dp % 8) // 2, dp % 2
    z_lo, core = me // 2, me % 2
    z = z_hi * SIDE + z_lo
    lanes = aligned((core * SIDE + z_lo) * HEAD, HEAD, HEAD)

    def pick(which_core, first, second):
        return first * (1 - which_core) + second * which_core

    rank, own_slot = pick(core, y, x), pick(core, x, y)
    z_right = place(y, x, (z + 1) % RING, core)
    z_left = place(y, x, (z + RING - 1) % RING, core)

    def along_x(k, which_core):
        return place(y, (x + k) % SIDE, z, which_core)

    def along_y(k, which_core):
        return place((y + k) % SIDE, x, z, which_core)

    def row_peer(k):
        return place(pick(core, (y + k) % SIDE, y), pick(core, x, (x + k) % SIDE), z, core)

    def weight_peer(k, which_core):
        return place(pick(which_core, y, (y + k) % SIDE), pick(which_core, (x + k) % SIDE, x), z, which_core)

    def remote(src, dst, send, recv, device):
        copy = pltpu.make_async_remote_copy(
            src_ref=src, dst_ref=dst, send_sem=send, recv_sem=recv, device_id=device, device_id_type=MESH
        )
        copy.start()
        return copy

    def wait_bytes(ref, sem):
        pltpu.make_async_copy(ref, ref, sem).wait()

    barrier = pltpu.get_barrier_semaphore()
    greeted = [(dp, (me + k) % NT) for k in range(1, NT)] + [z_right, z_left]
    for k in range(1, SIDE):
        greeted += [along_x(k, 0), along_x(k, 1), along_y(k, 0), along_y(k, 1)]
    for device in greeted:
        pl.semaphore_signal(barrier, inc=1, device_id=device, device_id_type=MESH)
    own_copies = [
        pltpu.make_async_copy(
            weight.at[:, pl.ds(j * HEAD, HEAD)],
            wbuf.at[j, aligned(own_slot * SLAB + z_hi * COLS, COLS, COLS), lanes],
            own_sem.at[0],
        )
        for j in range(PARTS)
    ]
    for copy in own_copies:
        copy.start()
    residual = [
        pltpu.make_async_copy(source, target, local_sem.at[i])
        for i, (source, target) in enumerate(
            ((hidden, hid), (hidden_tan, hid_tan), (gate_table, gates), (gate_rate, rates))
        )
    ]
    for copy in residual:
        copy.start()
    pl.semaphore_wait(barrier, len(greeted))

    def xor_peer(k):
        result = 0
        for bit in (1, 2, 4):
            mine = (me // bit) % 2
            result = result + bit * ((1 - mine) if k & bit else mine)
        return result

    peers = [xor_peer(k) for k in PEER_ORDER]

    def head_columns(peer, j):
        return aligned((peer * PARTS + j) * HEAD, HEAD, HEAD)

    def start_kv(j, half):
        source = (proj, ptan)[half]
        target = xkv.at[j, pl.ds(2 * half, 2), me]
        for peer in peers:
            remote(
                source.at[pl.ds(1, 2), :, :, head_columns(peer, j)],
                target,
                kv_send.at[j, half],
                kv_recv.at[j, half],
                (dp, peer),
            )
        pltpu.make_async_copy(
            source.at[pl.ds(1, 2), :, :, head_columns(me, j)], target, kv_recv.at[j, half]
        ).start()

    def wait_kv(j, half):
        wait_bytes(xkv.at[j, pl.ds(2 * half, 2)], kv_recv.at[j, half])

    def slot(j, group):
        return j if group is None else LAST + group

    def span(group):
        return pl.ds(*(ALL if group is None else GROUPS[group]))

    def start_q(j, group=None):
        blocks, i = span(group), slot(j, group)
        for peer in peers:
            for half, source in enumerate((proj, ptan)):
                remote(
                    source.at[0, blocks, :, head_columns(peer, j)],
                    xq.at[j, half, blocks, me],
                    q_send.at[i],
                    q_recv.at[i],
                    (dp, peer),
                )
        for half, source in enumerate((proj, ptan)):
            pltpu.make_async_copy(
                source.at[0, blocks, :, head_columns(me, j)], xq.at[j, half, blocks, me], q_recv.at[i]
            ).start()

    def wait_q(j, group=None):
        wait_bytes(xq.at[j, :, span(group)], q_recv.at[slot(j, group)])

    def start_back(j, group=None):
        blocks, i = span(group), slot(j, group)
        for peer in peers:
            remote(
                att.at[j, blocks, :, peer],
                tok.at[j, pick(peer % 2, y, x), blocks, :, :, lanes],
                back_send.at[i],
                back_recv.at[i],
                (dp, peer),
            )
        pltpu.make_async_copy(att.at[j, blocks, :, me], tok.at[j, rank, blocks, :, :, lanes], back_recv.at[i]).start()

    def start_tokens(j, group=None):
        i = slot(j, group)
        mine = tok.at[j, rank, span(group)]
        wait_bytes(mine, back_recv.at[i])
        for k in range(1, SIDE):
            remote(mine, mine, tok_send.at[i, k - 1], tok_recv.at[i, k - 1], row_peer(k))

    def wait_tokens(j, group=None):
        for k in range(1, SIDE):
            wait_bytes(tok.at[j, (rank + SIDE - k) % SIDE, span(group)], tok_recv.at[slot(j, group), k - 1])

    def attend(j, first, count):
        blocks, rows = pl.ds(first, count), count * NT * UNIT
        q = xq[j, 0, blocks].reshape(rows, HEAD)
        qt = xq[j, 1, blocks].reshape(rows, HEAD)
        k, v, kt, vt = (xkv[j, i].reshape(LEN, HEAD) for i in range(4))
        s = lax.dot_general(q, k, NT_DIMS, preferred_element_type=jnp.float32)
        st = lax.dot_general(
            jnp.concatenate([qt, q], axis=1),
            jnp.concatenate([k, kt], axis=1),
            NT_DIMS,
            preferred_element_type=jnp.float32,
        )
        top = jnp.max(s, axis=-1, keepdims=True)
        e = jnp.exp2((s - top) * (SCALE * math.log2(math.e)))
        probs = e * (1.0 / jnp.sum(e, axis=-1, keepdims=True))
        low = probs.astype(jnp.bfloat16)
        mean = jnp.sum(probs * st, axis=-1, keepdims=True)
        probs_tan = (probs * ((st - mean) * SCALE)).astype(jnp.bfloat16)
        both = jnp.dot(low, jnp.concatenate([v, vt], axis=1), preferred_element_type=jnp.float32)
        tan = jnp.dot(probs_tan, v, preferred_element_type=jnp.float32) + both[:, HEAD:]
        att[j, blocks, 0] = both[:, :HEAD].astype(jnp.bfloat16).reshape(count, NT, UNIT, HEAD)
        att[j, blocks, 1] = tan.astype(jnp.bfloat16).reshape(count, NT, UNIT, HEAD)

    def attend_all(j):
        attend(j, *ALL)

    def project(j):
        rows = tok[j].reshape(SIDE * 2 * ROWS, NT * HEAD)

        def tile(n, carry):
            part = lax.dot_general(
                rows,
                wbuf[j, aligned(n * TILE, TILE, TILE), :],
                NT_DIMS,
                preferred_element_type=jnp.float32,
            ).reshape(SIDE, BLOCKS, 2 * UNIT, TILE)
            if j == 0:
                acc[n] = part
            else:
                acc[n] = acc[n] + part
            return carry

        lax.fori_loop(0, TILES, tile, 0)

    def project_last(group):
        first, count = GROUPS[group]
        rows = tok[LAST, :, first : first + count].reshape(SIDE * count * 2 * UNIT, NT * HEAD)

        def tile(n, carry):
            part = lax.dot_general(
                rows,
                wbuf[LAST, aligned(n * TILE, TILE, TILE), :],
                NT_DIMS,
                preferred_element_type=jnp.float32,
            ).reshape(SIDE, count, 2 * UNIT, TILE)
            for b in range(count):
                total = (acc[n, :, first + b] + part[:, b]).astype(jnp.bfloat16)
                out_send[first + b, :, n] = total.reshape(SIDE, 2, UNIT, TILE)
            return carry

        lax.fori_loop(0, TILES, tile, 0)
        blocks = pl.ds(first, count)
        for k in range(1, SIDE):
            remote(
                out_send.at[blocks, (rank + k) % SIDE],
                out_recv.at[blocks, rank],
                res_send.at[group, k - 1],
                res_recv.at[group, k - 1],
                row_peer(k),
            )
        out_recv[blocks, rank] = out_send[blocks, rank]

    def shard(slot, which, parts=pl.ds(0, PARTS)):
        return wbuf.at[
            parts,
            aligned(slot * SLAB + (which // SIDE) * COLS, COLS, COLS),
            aligned((core * SIDE + which % SIDE) * HEAD, HEAD, HEAD),
        ]

    def slab(slot, which_core):
        return wbuf.at[
            :, aligned(slot * SLAB, SLAB, SLAB), aligned(which_core * SIDE * HEAD, SIDE * HEAD, SIDE * HEAD)
        ]

    def reach(which, direction):
        return (5 - which % SIDE) if direction == 0 else (2 + which % SIDE)

    def ring_copy(which, direction, s):
        piece = shard(own_slot, which)
        return pltpu.make_async_remote_copy(
            src_ref=piece,
            dst_ref=piece,
            send_sem=z_send.at[direction, s],
            recv_sem=z_recv.at[direction, s],
            device_id=(z_right, z_left)[direction],
            device_id_type=MESH,
        )

    def fan(which):
        source = shard(own_slot, which)
        for k in range(1, SIDE):
            remote(source, source, w_send.at[k - 1], w_recv.at[k - 1], weight_peer(k, core))
        other = shard(pick(core, y, x), which)
        for k in range(SIDE):
            remote(source, other, w_send.at[3 + k], w_recv.at[3 + k], weight_peer(k, 1 - core))

    def ring_wait(s):
        for direction in range(2):
            which = ((z + RING - s - 1) if direction == 0 else (z + s + 1)) % RING

            def arrived(which=which, direction=direction):
                wait_bytes(shard(own_slot, which), z_recv.at[direction, s])
                if s == 0:
                    ring_copy(which, direction, 1).start()
                elif s < 4:
                    pl.when(s + 1 < reach(which, direction))(lambda: ring_copy(which, direction, s + 1).start())
                fan(which)

            if s < 2:
                arrived()
            else:
                pl.when(s < reach(which, direction))(arrived)

    def wait_weights():
        for k in range(1, SIDE):
            wait_bytes(slab((own_slot + SIDE - k) % SIDE, core), w_recv.at[k - 1])
        for k in range(SIDE):
            wait_bytes(slab((own_slot + SIDE - k) % SIDE, 1 - core), w_recv.at[3 + k])

    wait_bytes(shard(own_slot, z), own_sem.at[0])
    for direction in range(2):
        ring_copy(z, direction, 0).start()
    start_kv(0, 0)
    start_kv(0, 1)
    start_q(0)
    fan(z)
    last = len(GROUPS)
    for j in range(PARTS - 1):
        for half in range(2):
            if 2 * j + half < 5:
                ring_wait(2 * j + half)
            wait_kv(j, half)
            start_kv(j + 1, half)
        wait_q(j)
        attend_all(j)
        start_back(j)
        if j + 1 < LAST:
            start_q(j + 1)
        if j >= 1:
            start_tokens(j - 1)
    wait_weights()
    for j in range(2):
        wait_tokens(j)
        project(j)
    wait_kv(LAST, 0)
    start_q(LAST, 0)
    wait_kv(LAST, 1)
    for group in range(1, last):
        start_q(LAST, group)
    start_tokens(3)
    wait_tokens(2)
    project(2)
    for group in range(last):
        wait_q(LAST, group)
        attend(LAST, *GROUPS[group])
        start_back(LAST, group)
        if group >= 1:
            start_tokens(LAST, group - 1)
    start_tokens(LAST, last - 1)
    wait_tokens(3)
    project(3)
    for group in range(last):
        wait_tokens(LAST, group)
        project_last(group)

    for copy in residual:
        copy.wait()
    level = timestep[0]
    levels = lax.broadcasted_iota(jnp.int32, gates.shape, 0)
    gate_row = jnp.sum(jnp.where(levels == level, gates[...], 0.0), axis=0, keepdims=True)
    rate_row = jnp.sum(jnp.where(levels == level, rates[...], 0.0), axis=0, keepdims=True)
    gates[0:1, :] = gate_row
    rates[0:1, :] = rate_row

    def finish(b, columns, value, value_tan):
        rows = pl.ds(b * UNIT, UNIT)
        gate, rate = gates[0:1, columns], rates[0:1, columns]
        out[rows, columns] = (hid[rows, columns].astype(jnp.float32) + gate * value).astype(jnp.bfloat16)
        out_tan[rows, columns] = (
            hid_tan[rows, columns].astype(jnp.float32) + gate * value_tan + rate * value
        ).astype(jnp.bfloat16)

    def finish_straight(b):
        for r in range(SIDE):
            for n in range(TILES):
                value = out_recv[b, r, n].astype(jnp.float32)
                finish(b, pl.ds(r * SLICE + n * TILE, TILE), value[0], value[1])

    def finish_crossed(b):
        lower = lax.broadcasted_iota(jnp.int32, (2 * UNIT, HEAD), 1) < HEAD // 2

        def load(r, unit):
            q = unit // 2
            piece = out_recv[b, r, q // 2, :, :, pl.ds((q % 2) * HEAD, HEAD)]
            return piece.astype(jnp.float32).reshape(2 * UNIT, HEAD)

        for t in range(D // HEAD):
            found = []
            for g in (2 * t, 2 * t + 1):
                s, rest = g // 20, g % 20
                found.append((rest // 5, 5 * s + rest % 5))
            (r0, u0), (r1, u1) = found
            first = load(r0, u0)
            if u0 % 2:
                first = pltpu.roll(first, HEAD // 2, 1)
            if r0 == r1 and u0 % 2 == 0 and u1 == u0 + 1:
                value = first
            else:
                second = load(r1, u1)
                if u1 % 2 == 0:
                    second = pltpu.roll(second, HEAD // 2, 1)
                value = jnp.where(lower, first, second)
            finish(b, pl.ds(t * HEAD, HEAD), value[:UNIT], value[UNIT:])

    for group, (first, count) in enumerate(GROUPS):
        for k in range(1, SIDE):
            wait_bytes(out_recv.at[pl.ds(first, count), (rank + SIDE - k) % SIDE], res_recv.at[group, k - 1])
        for b in range(first, first + count):
            pl.when(core == 0)(lambda b=b: finish_straight(b))
            pl.when(core == 1)(lambda b=b: finish_crossed(b))

    for j in range(PARTS):
        for half in range(2):
            wait_bytes(xkv.at[j, pl.ds(2 * half, 2), pl.ds(0, NT - 1)], kv_send.at[j, half])
        for group in (None,) if j < LAST else range(len(GROUPS)):
            blocks, i = span(group), slot(j, group)
            wait_bytes(xq.at[j, :, blocks, pl.ds(0, NT - 1)], q_send.at[i])
            wait_bytes(att.at[j, blocks, :, pl.ds(0, NT - 1)], back_send.at[i])
            for k in range(SIDE - 1):
                wait_bytes(tok.at[j, rank, blocks], tok_send.at[i, k])
    for direction in range(2):
        for s in range(5):
            which = ((z + RING - s) if direction == 0 else (z + s)) % RING
            done = lambda which=which, direction=direction, s=s: ring_copy(which, direction, s).wait_send()
            if s < 2:
                done()
            else:
                pl.when(s < reach(which, direction))(done)
    for k in range(7):
        wait_bytes(slab(own_slot, core), w_send.at[k])
    for group, (first, count) in enumerate(GROUPS):
        for k in range(SIDE - 1):
            wait_bytes(out_send.at[pl.ds(first, count), 0], res_send.at[group, k])


def shards(projected, projected_tan, hidden, hidden_tan, out_weight, gate_table, gate_rate, timestep):
    proj = jnp.transpose(projected, (0, 2, 1, 3)).reshape(3, BLOCKS, UNIT, D)
    ptan = jnp.transpose(projected_tan, (0, 2, 1, 3)).reshape(3, BLOCKS, UNIT, D)
    any_spec = pl.BlockSpec(memory_space=pl.ANY)
    vmem = pl.BlockSpec(memory_space=pltpu.VMEM)
    bf16 = jnp.bfloat16
    dma = pltpu.SemaphoreType.DMA
    block_out, block_tan = pl.pallas_call(
        kernel,
        out_shape=(jax.ShapeDtypeStruct((ROWS, D), bf16), jax.ShapeDtypeStruct((ROWS, D), bf16)),
        in_specs=[any_spec] * 7 + [pl.BlockSpec(memory_space=pltpu.SMEM)],
        out_specs=(vmem, vmem),
        scratch_shapes=[
            pltpu.VMEM((PARTS, 4, NT, BLOCKS, UNIT, HEAD), bf16),
            pltpu.VMEM((PARTS, 2, BLOCKS, NT, UNIT, HEAD), bf16),
            pltpu.VMEM((PARTS, BLOCKS, 2, NT, UNIT, HEAD), bf16),
            pltpu.VMEM((PARTS, SIDE, BLOCKS, 2, UNIT, NT * HEAD), bf16),
            pltpu.VMEM((PARTS, SLICE, NT * HEAD), bf16),
            pltpu.VMEM((TILES, SIDE, BLOCKS, 2 * UNIT, TILE), jnp.float32),
            pltpu.VMEM((BLOCKS, SIDE, TILES, 2, UNIT, TILE), bf16),
            pltpu.VMEM((BLOCKS, SIDE, TILES, 2, UNIT, TILE), bf16),
            pltpu.VMEM((ROWS, D), bf16),
            pltpu.VMEM((ROWS, D), bf16),
            pltpu.VMEM((32, D), jnp.float32),
            pltpu.VMEM((32, D), jnp.float32),
            dma((PARTS, 2)),
            dma((PARTS, 2)),
            dma((LAST + len(GROUPS),)),
            dma((LAST + len(GROUPS),)),
            dma((LAST + len(GROUPS),)),
            dma((LAST + len(GROUPS),)),
            dma((LAST + len(GROUPS), SIDE - 1)),
            dma((LAST + len(GROUPS), SIDE - 1)),
            dma((2, 5)),
            dma((2, 5)),
            dma((7,)),
            dma((7,)),
            dma((len(GROUPS), SIDE - 1)),
            dma((len(GROUPS), SIDE - 1)),
            dma((4,)),
            dma((1,)),
        ],
        compiler_params=pltpu.CompilerParams(
            collective_id=0, has_side_effects=True, vmem_limit_bytes=56 * 1024 * 1024
        ),
    )(
        proj,
        ptan,
        hidden.reshape(ROWS, D),
        hidden_tan.reshape(ROWS, D),
        out_weight.T,
        gate_table,
        gate_rate,
        timestep,
    )
    return block_out[None], block_tan[None]


def solution(mesh):
    return jax.shard_map(
        shards,
        mesh=mesh,
        in_specs=(
            P("dp", "tensor", None, None),
            P("dp", "tensor", None, None),
            P("dp", "tensor", None),
            P("dp", "tensor", None),
            P("tensor", "dp"),
            P(),
            P(),
            P("dp"),
        ),
        out_specs=(P("dp", "tensor", None), P("dp", "tensor", None)),
        check_vma=False,
    )
```

```python
import math

import jax
import jax.numpy as jnp
from jax import lax
from jax.experimental import pallas as pl
from jax.experimental.pallas import tpu as pltpu
from jax.sharding import PartitionSpec as P

HEAD = 128
PARTS = 5
LEN = 512
ROWS = 64
BLOCKS = 4
UNIT = ROWS // BLOCKS
ALL = (0, BLOCKS)
GROUPS = ((0, 2), (2, 2))
OUT_GROUPS = ((0, 2), (2, 2))
LAST = 4
NT = 8
SIDE = 4
RING = 8
COLS = 160
SLAB = 320
SLICE = 1280
TILES = 5
TILE = 256
D = 5120
PEER_ORDER = (2, 3, 4, 5, 6, 7, 1)
SCALE = 1.0 / math.sqrt(HEAD)
MESH = pl.DeviceIdType.MESH
NT_DIMS = (((1,), (1,)), ((), ()))


def place(y, x, z, core):
    return (y * 8 + x * 2 + z // SIDE, (z % SIDE) * 2 + core)


def aligned(value, size, base):
    return pl.ds(pl.multiple_of(value, base), size)


def kernel(
    proj, ptan, hidden, hidden_tan, weight, gate_table, gate_rate, timestep,
    out, out_tan,
    xkv, xq, att, tok, wbuf, acc, out_send, out_recv, hid, hid_tan, gates, rates,
    kv_send, kv_recv, q_send, q_recv, back_send, back_recv, tok_send, tok_recv,
    z_send, z_recv, w_send, w_recv, res_send, res_recv, local_sem, own_sem,
):
    dp, me = lax.axis_index("dp"), lax.axis_index("tensor")
    y, x, z_hi = dp // 8, (dp % 8) // 2, dp % 2
    z_lo, core = me // 2, me % 2
    z = z_hi * SIDE + z_lo
    lanes = aligned((core * SIDE + z_lo) * HEAD, HEAD, HEAD)

    def pick(which_core, first, second):
        return first * (1 - which_core) + second * which_core

    rank, own_slot = pick(core, y, x), pick(core, x, y)
    z_right = place(y, x, (z + 1) % RING, core)
    z_left = place(y, x, (z + RING - 1) % RING, core)

    def along_x(k, which_core):
        return place(y, (x + k) % SIDE, z, which_core)

    def along_y(k, which_core):
        return place((y + k) % SIDE, x, z, which_core)

    def row_peer(k):
        return place(pick(core, (y + k) % SIDE, y), pick(core, x, (x + k) % SIDE), z, core)

    def weight_peer(k, which_core):
        return place(pick(which_core, y, (y + k) % SIDE), pick(which_core, (x + k) % SIDE, x), z, which_core)

    def remote(src, dst, send, recv, device):
        copy = pltpu.make_async_remote_copy(
            src_ref=src, dst_ref=dst, send_sem=send, recv_sem=recv, device_id=device, device_id_type=MESH
        )
        copy.start()
        return copy

    def wait_bytes(ref, sem):
        pltpu.make_async_copy(ref, ref, sem).wait()

    barrier = pltpu.get_barrier_semaphore()
    greeted = [(dp, (me + k) % NT) for k in range(1, NT)] + [z_right, z_left]
    for k in range(1, SIDE):
        greeted += [along_x(k, 0), along_x(k, 1), along_y(k, 0), along_y(k, 1)]
    for device in greeted:
        pl.semaphore_signal(barrier, inc=1, device_id=device, device_id_type=MESH)
    own_copies = [
        pltpu.make_async_copy(
            weight.at[:, pl.ds(j * HEAD, HEAD)],
            wbuf.at[j, aligned(own_slot * SLAB + z_hi * COLS, COLS, COLS), lanes],
            own_sem.at[0],
        )
        for j in range(PARTS)
    ]
    for copy in own_copies:
        copy.start()
    residual = [
        pltpu.make_async_copy(source, target, local_sem.at[i])
        for i, (source, target) in enumerate(
            ((hidden, hid), (hidden_tan, hid_tan), (gate_table, gates), (gate_rate, rates))
        )
    ]
    for copy in residual:
        copy.start()
    pl.semaphore_wait(barrier, len(greeted))

    def xor_peer(k):
        result = 0
        for bit in (1, 2, 4):
            mine = (me // bit) % 2
            result = result + bit * ((1 - mine) if k & bit else mine)
        return result

    peers = [xor_peer(k) for k in PEER_ORDER]

    def head_columns(peer, j):
        return aligned((peer * PARTS + j) * HEAD, HEAD, HEAD)

    def start_kv(j, half):
        source = (proj, ptan)[half]
        target = xkv.at[j, pl.ds(2 * half, 2), me]
        for peer in peers:
            remote(
                source.at[pl.ds(1, 2), :, :, head_columns(peer, j)],
                target,
                kv_send.at[j, half],
                kv_recv.at[j, half],
                (dp, peer),
            )
        pltpu.make_async_copy(
            source.at[pl.ds(1, 2), :, :, head_columns(me, j)], target, kv_recv.at[j, half]
        ).start()

    def wait_kv(j, half):
        wait_bytes(xkv.at[j, pl.ds(2 * half, 2)], kv_recv.at[j, half])

    def slot(j, group):
        return j if group is None else LAST + group

    def span(group):
        return pl.ds(*(ALL if group is None else GROUPS[group]))

    def start_q(j, group=None):
        blocks, i = span(group), slot(j, group)
        for peer in peers:
            for half, source in enumerate((proj, ptan)):
                remote(
                    source.at[0, blocks, :, head_columns(peer, j)],
                    xq.at[j, half, blocks, me],
                    q_send.at[i],
                    q_recv.at[i],
                    (dp, peer),
                )
        for half, source in enumerate((proj, ptan)):
            pltpu.make_async_copy(
                source.at[0, blocks, :, head_columns(me, j)], xq.at[j, half, blocks, me], q_recv.at[i]
            ).start()

    def wait_q(j, group=None):
        wait_bytes(xq.at[j, :, span(group)], q_recv.at[slot(j, group)])

    def start_back(j, group=None):
        blocks, i = span(group), slot(j, group)
        for peer in peers:
            remote(
                att.at[j, blocks, :, peer],
                tok.at[j, pick(peer % 2, y, x), blocks, :, :, lanes],
                back_send.at[i],
                back_recv.at[i],
                (dp, peer),
            )
        pltpu.make_async_copy(att.at[j, blocks, :, me], tok.at[j, rank, blocks, :, :, lanes], back_recv.at[i]).start()

    def start_tokens(j, group=None):
        i = slot(j, group)
        mine = tok.at[j, rank, span(group)]
        wait_bytes(mine, back_recv.at[i])
        for k in (2, 1, 3):
            remote(mine, mine, tok_send.at[i, k - 1], tok_recv.at[i, k - 1], row_peer(k))

    def wait_tokens(j, group=None):
        for k in range(1, SIDE):
            wait_bytes(tok.at[j, (rank + SIDE - k) % SIDE, span(group)], tok_recv.at[slot(j, group), k - 1])

    def attend(j, first, count):
        blocks, rows = pl.ds(first, count), count * NT * UNIT
        q = xq[j, 0, blocks].reshape(rows, HEAD)
        qt = xq[j, 1, blocks].reshape(rows, HEAD)
        k, v, kt, vt = (xkv[j, i].reshape(LEN, HEAD) for i in range(4))
        s = lax.dot_general(q, k, NT_DIMS, preferred_element_type=jnp.float32)
        st = lax.dot_general(
            jnp.concatenate([qt, q], axis=1),
            jnp.concatenate([k, kt], axis=1),
            NT_DIMS,
            preferred_element_type=jnp.float32,
        )
        top = jnp.max(s, axis=-1, keepdims=True)
        e = jnp.exp2((s - top) * (SCALE * math.log2(math.e)))
        probs = e * (1.0 / jnp.sum(e, axis=-1, keepdims=True))
        low = probs.astype(jnp.bfloat16)
        mean = jnp.sum(probs * st, axis=-1, keepdims=True)
        probs_tan = (probs * ((st - mean) * SCALE)).astype(jnp.bfloat16)
        both = jnp.dot(low, jnp.concatenate([v, vt], axis=1), preferred_element_type=jnp.float32)
        tan = jnp.dot(probs_tan, v, preferred_element_type=jnp.float32) + both[:, HEAD:]
        att[j, blocks, 0] = both[:, :HEAD].astype(jnp.bfloat16).reshape(count, NT, UNIT, HEAD)
        att[j, blocks, 1] = tan.astype(jnp.bfloat16).reshape(count, NT, UNIT, HEAD)

    def attend_all(j):
        attend(j, *ALL)

    def project(j):
        rows = tok[j].reshape(SIDE * 2 * ROWS, NT * HEAD)

        def tile(n, carry):
            part = lax.dot_general(
                rows,
                wbuf[j, aligned(n * TILE, TILE, TILE), :],
                NT_DIMS,
                preferred_element_type=jnp.float32,
            ).reshape(SIDE, BLOCKS, 2 * UNIT, TILE)
            if j == 0:
                acc[n] = part
            else:
                acc[n] = acc[n] + part
            return carry

        lax.fori_loop(0, TILES, tile, 0)

    def project_last(group):
        first, count = OUT_GROUPS[group]
        rows = tok[LAST, :, first : first + count].reshape(SIDE * count * 2 * UNIT, NT * HEAD)

        def tile(n, carry):
            part = lax.dot_general(
                rows,
                wbuf[LAST, aligned(n * TILE, TILE, TILE), :],
                NT_DIMS,
                preferred_element_type=jnp.float32,
            ).reshape(SIDE, count, 2 * UNIT, TILE)
            for b in range(count):
                total = (acc[n, :, first + b] + part[:, b]).astype(jnp.bfloat16)
                out_send[first + b, :, n] = total.reshape(SIDE, 2, UNIT, TILE)
            return carry

        lax.fori_loop(0, TILES, tile, 0)
        blocks = pl.ds(first, count)
        for k in (2, 1, 3):
            remote(
                out_send.at[blocks, (rank + k) % SIDE],
                out_recv.at[blocks, rank],
                res_send.at[group, k - 1],
                res_recv.at[group, k - 1],
                row_peer(k),
            )
        out_recv[blocks, rank] = out_send[blocks, rank]

    def shard(slot, which, parts=pl.ds(0, PARTS)):
        return wbuf.at[
            parts,
            aligned(slot * SLAB + (which // SIDE) * COLS, COLS, COLS),
            aligned((core * SIDE + which % SIDE) * HEAD, HEAD, HEAD),
        ]

    def slab(slot, which_core):
        return wbuf.at[
            :, aligned(slot * SLAB, SLAB, SLAB), aligned(which_core * SIDE * HEAD, SIDE * HEAD, SIDE * HEAD)
        ]

    def reach(which, direction):
        return (5 - which % SIDE) if direction == 0 else (2 + which % SIDE)

    def ring_copy(which, direction, s):
        piece = shard(own_slot, which)
        return pltpu.make_async_remote_copy(
            src_ref=piece,
            dst_ref=piece,
            send_sem=z_send.at[direction, s],
            recv_sem=z_recv.at[direction, s],
            device_id=(z_right, z_left)[direction],
            device_id_type=MESH,
        )

    def fan(which):
        source = shard(own_slot, which)
        for k in range(1, SIDE):
            remote(source, source, w_send.at[k - 1], w_recv.at[k - 1], weight_peer(k, core))
        other = shard(pick(core, y, x), which)
        for k in range(SIDE):
            remote(source, other, w_send.at[3 + k], w_recv.at[3 + k], weight_peer(k, 1 - core))

    def ring_wait(s):
        for direction in range(2):
            which = ((z + RING - s - 1) if direction == 0 else (z + s + 1)) % RING

            def arrived(which=which, direction=direction):
                wait_bytes(shard(own_slot, which), z_recv.at[direction, s])
                if s == 0:
                    ring_copy(which, direction, 1).start()
                elif s < 4:
                    pl.when(s + 1 < reach(which, direction))(lambda: ring_copy(which, direction, s + 1).start())
                fan(which)

            if s < 2:
                arrived()
            else:
                pl.when(s < reach(which, direction))(arrived)

    def wait_weights():
        for k in range(1, SIDE):
            wait_bytes(slab((own_slot + SIDE - k) % SIDE, core), w_recv.at[k - 1])
        for k in range(SIDE):
            wait_bytes(slab((own_slot + SIDE - k) % SIDE, 1 - core), w_recv.at[3 + k])

    wait_bytes(shard(own_slot, z), own_sem.at[0])
    for direction in range(2):
        ring_copy(z, direction, 0).start()
    start_kv(0, 0)
    start_kv(0, 1)
    start_q(0)
    fan(z)
    last = len(GROUPS)
    for j in range(PARTS - 1):
        for half in range(2):
            if 2 * j + half < 5:
                ring_wait(2 * j + half)
            wait_kv(j, half)
            if j + 1 < LAST or half == 0:
                start_kv(j + 1, half)
        wait_q(j)
        attend_all(j)
        start_back(j)
        if j + 1 == LAST:
            start_kv(LAST, 1)
        if j + 1 < LAST:
            start_q(j + 1)
        if j >= 1:
            start_tokens(j - 1)
    for copy in residual:
        copy.wait()
    level = timestep[0]
    levels = lax.broadcasted_iota(jnp.int32, gates.shape, 0)
    gate_row = jnp.sum(jnp.where(levels == level, gates[...], 0.0), axis=0, keepdims=True)
    rate_row = jnp.sum(jnp.where(levels == level, rates[...], 0.0), axis=0, keepdims=True)
    gates[0:1, :] = gate_row
    rates[0:1, :] = rate_row

    wait_weights()
    for j in range(2):
        wait_tokens(j)
        project(j)
    wait_kv(LAST, 0)
    start_q(LAST, 0)
    wait_kv(LAST, 1)
    for group in range(1, last):
        start_q(LAST, group)
    start_tokens(3)
    wait_tokens(2)
    project(2)
    for group in range(last):
        wait_q(LAST, group)
        attend(LAST, *GROUPS[group])
        start_back(LAST, group)
    for group in range(last):
        start_tokens(LAST, group)
        if group == 0:
            wait_tokens(3)
            project(3)
    arrived = 0
    for group, (first, count) in enumerate(OUT_GROUPS):
        while arrived < last and GROUPS[arrived][0] < first + count:
            wait_tokens(LAST, arrived)
            arrived += 1
        project_last(group)

    def finish(b, columns, value, value_tan):
        rows = pl.ds(b * UNIT, UNIT)
        gate, rate = gates[0:1, columns], rates[0:1, columns]
        out[rows, columns] = (hid[rows, columns].astype(jnp.float32) + gate * value).astype(jnp.bfloat16)
        out_tan[rows, columns] = (
            hid_tan[rows, columns].astype(jnp.float32) + gate * value_tan + rate * value
        ).astype(jnp.bfloat16)

    def finish_straight(b):
        for r in range(SIDE):
            for n in range(TILES):
                value = out_recv[b, r, n].astype(jnp.float32)
                finish(b, pl.ds(r * SLICE + n * TILE, TILE), value[0], value[1])

    def finish_crossed(b):
        lower = lax.broadcasted_iota(jnp.int32, (2 * UNIT, HEAD), 1) < HEAD // 2

        def load(r, unit):
            q = unit // 2
            piece = out_recv[b, r, q // 2, :, :, pl.ds((q % 2) * HEAD, HEAD)]
            return piece.astype(jnp.float32).reshape(2 * UNIT, HEAD)

        for t in range(D // HEAD):
            found = []
            for g in (2 * t, 2 * t + 1):
                s, rest = g // 20, g % 20
                found.append((rest // 5, 5 * s + rest % 5))
            (r0, u0), (r1, u1) = found
            first = load(r0, u0)
            if u0 % 2:
                first = pltpu.roll(first, HEAD // 2, 1)
            if r0 == r1 and u0 % 2 == 0 and u1 == u0 + 1:
                value = first
            else:
                second = load(r1, u1)
                if u1 % 2 == 0:
                    second = pltpu.roll(second, HEAD // 2, 1)
                value = jnp.where(lower, first, second)
            finish(b, pl.ds(t * HEAD, HEAD), value[:UNIT], value[UNIT:])

    for group, (first, count) in enumerate(OUT_GROUPS):
        for k in range(1, SIDE):
            wait_bytes(out_recv.at[pl.ds(first, count), (rank + SIDE - k) % SIDE], res_recv.at[group, k - 1])
        for b in range(first, first + count):
            pl.when(core == 0)(lambda b=b: finish_straight(b))
            pl.when(core == 1)(lambda b=b: finish_crossed(b))

    for j in range(PARTS):
        for half in range(2):
            wait_bytes(xkv.at[j, pl.ds(2 * half, 2), pl.ds(0, NT - 1)], kv_send.at[j, half])
        for group in (None,) if j < LAST else range(len(GROUPS)):
            blocks, i = span(group), slot(j, group)
            wait_bytes(xq.at[j, :, blocks, pl.ds(0, NT - 1)], q_send.at[i])
            wait_bytes(att.at[j, blocks, :, pl.ds(0, NT - 1)], back_send.at[i])
            for k in range(SIDE - 1):
                wait_bytes(tok.at[j, rank, blocks], tok_send.at[i, k])
    for direction in range(2):
        for s in range(5):
            which = ((z + RING - s) if direction == 0 else (z + s)) % RING
            done = lambda which=which, direction=direction, s=s: ring_copy(which, direction, s).wait_send()
            if s < 2:
                done()
            else:
                pl.when(s < reach(which, direction))(done)
    for k in range(7):
        wait_bytes(slab(own_slot, core), w_send.at[k])
    for group, (first, count) in enumerate(OUT_GROUPS):
        for k in range(SIDE - 1):
            wait_bytes(out_send.at[pl.ds(first, count), 0], res_send.at[group, k])


def shards(projected, projected_tan, hidden, hidden_tan, out_weight, gate_table, gate_rate, timestep):
    proj = jnp.transpose(projected, (0, 2, 1, 3)).reshape(3, BLOCKS, UNIT, D)
    ptan = jnp.transpose(projected_tan, (0, 2, 1, 3)).reshape(3, BLOCKS, UNIT, D)
    any_spec = pl.BlockSpec(memory_space=pl.ANY)
    vmem = pl.BlockSpec(memory_space=pltpu.VMEM)
    bf16 = jnp.bfloat16
    dma = pltpu.SemaphoreType.DMA
    block_out, block_tan = pl.pallas_call(
        kernel,
        out_shape=(jax.ShapeDtypeStruct((ROWS, D), bf16), jax.ShapeDtypeStruct((ROWS, D), bf16)),
        in_specs=[any_spec] * 7 + [pl.BlockSpec(memory_space=pltpu.SMEM)],
        out_specs=(vmem, vmem),
        scratch_shapes=[
            pltpu.VMEM((PARTS, 4, NT, BLOCKS, UNIT, HEAD), bf16),
            pltpu.VMEM((PARTS, 2, BLOCKS, NT, UNIT, HEAD), bf16),
            pltpu.VMEM((PARTS, BLOCKS, 2, NT, UNIT, HEAD), bf16),
            pltpu.VMEM((PARTS, SIDE, BLOCKS, 2, UNIT, NT * HEAD), bf16),
            pltpu.VMEM((PARTS, SLICE, NT * HEAD), bf16),
            pltpu.VMEM((TILES, SIDE, BLOCKS, 2 * UNIT, TILE), jnp.float32),
            pltpu.VMEM((BLOCKS, SIDE, TILES, 2, UNIT, TILE), bf16),
            pltpu.VMEM((BLOCKS, SIDE, TILES, 2, UNIT, TILE), bf16),
            pltpu.VMEM((ROWS, D), bf16),
            pltpu.VMEM((ROWS, D), bf16),
            pltpu.VMEM((32, D), jnp.float32),
            pltpu.VMEM((32, D), jnp.float32),
            dma((PARTS, 2)),
            dma((PARTS, 2)),
            dma((LAST + len(GROUPS),)),
            dma((LAST + len(GROUPS),)),
            dma((LAST + len(GROUPS),)),
            dma((LAST + len(GROUPS),)),
            dma((LAST + len(GROUPS), SIDE - 1)),
            dma((LAST + len(GROUPS), SIDE - 1)),
            dma((2, 5)),
            dma((2, 5)),
            dma((7,)),
            dma((7,)),
            dma((len(OUT_GROUPS), SIDE - 1)),
            dma((len(OUT_GROUPS), SIDE - 1)),
            dma((4,)),
            dma((1,)),
        ],
        compiler_params=pltpu.CompilerParams(
            collective_id=0, has_side_effects=True, vmem_limit_bytes=56 * 1024 * 1024
        ),
    )(
        proj,
        ptan,
        hidden.reshape(ROWS, D),
        hidden_tan.reshape(ROWS, D),
        out_weight.T,
        gate_table,
        gate_rate,
        timestep,
    )
    return block_out[None], block_tan[None]


def solution(mesh):
    return jax.shard_map(
        shards,
        mesh=mesh,
        in_specs=(
            P("dp", "tensor", None, None),
            P("dp", "tensor", None, None),
            P("dp", "tensor", None),
            P("dp", "tensor", None),
            P("tensor", "dp"),
            P(),
            P(),
            P("dp"),
        ),
        out_specs=(P("dp", "tensor", None), P("dp", "tensor", None)),
        check_vma=False,
    )
```

```python
import math

import jax
import jax.numpy as jnp
from jax import lax
from jax.experimental import pallas as pl
from jax.experimental.pallas import tpu as pltpu
from jax.sharding import PartitionSpec as P

HEAD = 128
PARTS = 5
LEN = 512
ROWS = 64
BLOCKS = 4
UNIT = ROWS // BLOCKS
ALL = (0, BLOCKS)
GROUPS = ((0, 2), (2, 2))
OUT_GROUPS = ((0, 2), (2, 2))
LAST = 4
NT = 8
SIDE = 4
RING = 8
COLS = 160
SLAB = 320
SLICE = 1280
TILES = 5
TILE = 256
D = 5120
PEER_ORDER = (2, 3, 4, 5, 6, 7, 1)
SCALE = 1.0 / math.sqrt(HEAD)
MESH = pl.DeviceIdType.MESH
NT_DIMS = (((1,), (1,)), ((), ()))


def place(y, x, z, core):
    return (y * 8 + x * 2 + z // SIDE, (z % SIDE) * 2 + core)


def aligned(value, size, base):
    return pl.ds(pl.multiple_of(value, base), size)


def kernel(
    proj, ptan, weight, gate_table, gate_rate, timestep,
    change,
    xkv, xq, att, tok, wbuf, acc, out_send, out_recv, gates, rates,
    kv_send, kv_recv, q_send, q_recv, back_send, back_recv, tok_send, tok_recv,
    z_send, z_recv, w_send, w_recv, res_send, res_recv, local_sem, own_sem,
):
    dp, me = lax.axis_index("dp"), lax.axis_index("tensor")
    y, x, z_hi = dp // 8, (dp % 8) // 2, dp % 2
    z_lo, core = me // 2, me % 2
    z = z_hi * SIDE + z_lo
    lanes = aligned((core * SIDE + z_lo) * HEAD, HEAD, HEAD)

    def pick(which_core, first, second):
        return first * (1 - which_core) + second * which_core

    rank, own_slot = pick(core, y, x), pick(core, x, y)
    z_right = place(y, x, (z + 1) % RING, core)
    z_left = place(y, x, (z + RING - 1) % RING, core)

    def along_x(k, which_core):
        return place(y, (x + k) % SIDE, z, which_core)

    def along_y(k, which_core):
        return place((y + k) % SIDE, x, z, which_core)

    def row_peer(k):
        return place(pick(core, (y + k) % SIDE, y), pick(core, x, (x + k) % SIDE), z, core)

    def weight_peer(k, which_core):
        return place(pick(which_core, y, (y + k) % SIDE), pick(which_core, (x + k) % SIDE, x), z, which_core)

    def remote(src, dst, send, recv, device):
        copy = pltpu.make_async_remote_copy(
            src_ref=src, dst_ref=dst, send_sem=send, recv_sem=recv, device_id=device, device_id_type=MESH
        )
        copy.start()
        return copy

    def wait_bytes(ref, sem):
        pltpu.make_async_copy(ref, ref, sem).wait()

    barrier = pltpu.get_barrier_semaphore()
    greeted = [(dp, (me + k) % NT) for k in range(1, NT)] + [z_right, z_left]
    for k in range(1, SIDE):
        greeted += [along_x(k, 0), along_x(k, 1), along_y(k, 0), along_y(k, 1)]
    for device in greeted:
        pl.semaphore_signal(barrier, inc=1, device_id=device, device_id_type=MESH)
    own_copies = [
        pltpu.make_async_copy(
            weight.at[:, pl.ds(j * HEAD, HEAD)],
            wbuf.at[j, aligned(own_slot * SLAB + z_hi * COLS, COLS, COLS), lanes],
            own_sem.at[0],
        )
        for j in range(PARTS)
    ]
    for copy in own_copies:
        copy.start()
    residual = [
        pltpu.make_async_copy(source, target, local_sem.at[i])
        for i, (source, target) in enumerate(
            ((gate_table, gates), (gate_rate, rates))
        )
    ]
    for copy in residual:
        copy.start()
    pl.semaphore_wait(barrier, len(greeted))

    def xor_peer(k):
        result = 0
        for bit in (1, 2, 4):
            mine = (me // bit) % 2
            result = result + bit * ((1 - mine) if k & bit else mine)
        return result

    peers = [xor_peer(k) for k in PEER_ORDER]

    def head_columns(peer, j):
        return aligned((peer * PARTS + j) * HEAD, HEAD, HEAD)

    def start_kv(j, half):
        source = (proj, ptan)[half]
        target = xkv.at[j, pl.ds(2 * half, 2), me]
        for peer in peers:
            remote(
                source.at[pl.ds(1, 2), :, :, head_columns(peer, j)],
                target,
                kv_send.at[j, half],
                kv_recv.at[j, half],
                (dp, peer),
            )
        pltpu.make_async_copy(
            source.at[pl.ds(1, 2), :, :, head_columns(me, j)], target, kv_recv.at[j, half]
        ).start()

    def wait_kv(j, half):
        wait_bytes(xkv.at[j, pl.ds(2 * half, 2)], kv_recv.at[j, half])

    def slot(j, group):
        return j if group is None else LAST + group

    def span(group):
        return pl.ds(*(ALL if group is None else GROUPS[group]))

    def start_q(j, group=None):
        blocks, i = span(group), slot(j, group)
        for peer in peers:
            for half, source in enumerate((proj, ptan)):
                remote(
                    source.at[0, blocks, :, head_columns(peer, j)],
                    xq.at[j, half, blocks, me],
                    q_send.at[i],
                    q_recv.at[i],
                    (dp, peer),
                )
        for half, source in enumerate((proj, ptan)):
            pltpu.make_async_copy(
                source.at[0, blocks, :, head_columns(me, j)], xq.at[j, half, blocks, me], q_recv.at[i]
            ).start()

    def wait_q(j, group=None):
        wait_bytes(xq.at[j, :, span(group)], q_recv.at[slot(j, group)])

    def start_back(j, group=None):
        blocks, i = span(group), slot(j, group)
        for peer in peers:
            remote(
                att.at[j, blocks, :, peer],
                tok.at[j, pick(peer % 2, y, x), blocks, :, :, lanes],
                back_send.at[i],
                back_recv.at[i],
                (dp, peer),
            )
        pltpu.make_async_copy(att.at[j, blocks, :, me], tok.at[j, rank, blocks, :, :, lanes], back_recv.at[i]).start()

    def start_tokens(j, group=None):
        i = slot(j, group)
        mine = tok.at[j, rank, span(group)]
        wait_bytes(mine, back_recv.at[i])
        for k in (2, 1, 3):
            remote(mine, mine, tok_send.at[i, k - 1], tok_recv.at[i, k - 1], row_peer(k))

    def wait_tokens(j, group=None):
        for k in range(1, SIDE):
            wait_bytes(tok.at[j, (rank + SIDE - k) % SIDE, span(group)], tok_recv.at[slot(j, group), k - 1])

    def attend(j, first, count):
        blocks, rows = pl.ds(first, count), count * NT * UNIT
        q = xq[j, 0, blocks].reshape(rows, HEAD)
        qt = xq[j, 1, blocks].reshape(rows, HEAD)
        k, v, kt, vt = (xkv[j, i].reshape(LEN, HEAD) for i in range(4))
        s = lax.dot_general(q, k, NT_DIMS, preferred_element_type=jnp.float32)
        st = lax.dot_general(
            jnp.concatenate([qt, q], axis=1),
            jnp.concatenate([k, kt], axis=1),
            NT_DIMS,
            preferred_element_type=jnp.float32,
        )
        top = jnp.max(s, axis=-1, keepdims=True)
        e = jnp.exp2((s - top) * (SCALE * math.log2(math.e)))
        probs = e * (1.0 / jnp.sum(e, axis=-1, keepdims=True))
        low = probs.astype(jnp.bfloat16)
        mean = jnp.sum(probs * st, axis=-1, keepdims=True)
        probs_tan = (probs * ((st - mean) * SCALE)).astype(jnp.bfloat16)
        both = jnp.dot(low, jnp.concatenate([v, vt], axis=1), preferred_element_type=jnp.float32)
        tan = jnp.dot(probs_tan, v, preferred_element_type=jnp.float32) + both[:, HEAD:]
        att[j, blocks, 0] = both[:, :HEAD].astype(jnp.bfloat16).reshape(count, NT, UNIT, HEAD)
        att[j, blocks, 1] = tan.astype(jnp.bfloat16).reshape(count, NT, UNIT, HEAD)

    def attend_all(j):
        attend(j, *ALL)

    def project(j):
        rows = tok[j].reshape(SIDE * 2 * ROWS, NT * HEAD)

        def tile(n, carry):
            part = lax.dot_general(
                rows,
                wbuf[j, aligned(n * TILE, TILE, TILE), :],
                NT_DIMS,
                preferred_element_type=jnp.float32,
            ).reshape(SIDE, BLOCKS, 2 * UNIT, TILE)
            if j == 0:
                acc[n] = part
            else:
                acc[n] = acc[n] + part
            return carry

        lax.fori_loop(0, TILES, tile, 0)

    def project_last(group):
        first, count = OUT_GROUPS[group]
        rows = tok[LAST, :, first : first + count].reshape(SIDE * count * 2 * UNIT, NT * HEAD)

        def tile(n, carry):
            part = lax.dot_general(
                rows,
                wbuf[LAST, aligned(n * TILE, TILE, TILE), :],
                NT_DIMS,
                preferred_element_type=jnp.float32,
            ).reshape(SIDE, count, 2 * UNIT, TILE)
            for b in range(count):
                total = (acc[n, :, first + b] + part[:, b]).astype(jnp.bfloat16)
                out_send[first + b, :, n] = total.reshape(SIDE, 2, UNIT, TILE)
            return carry

        lax.fori_loop(0, TILES, tile, 0)
        blocks = pl.ds(first, count)
        for k in (2, 1, 3):
            remote(
                out_send.at[blocks, (rank + k) % SIDE],
                out_recv.at[blocks, rank],
                res_send.at[group, k - 1],
                res_recv.at[group, k - 1],
                row_peer(k),
            )
        out_recv[blocks, rank] = out_send[blocks, rank]

    def shard(slot, which, parts=pl.ds(0, PARTS)):
        return wbuf.at[
            parts,
            aligned(slot * SLAB + (which // SIDE) * COLS, COLS, COLS),
            aligned((core * SIDE + which % SIDE) * HEAD, HEAD, HEAD),
        ]

    def slab(slot, which_core):
        return wbuf.at[
            :, aligned(slot * SLAB, SLAB, SLAB), aligned(which_core * SIDE * HEAD, SIDE * HEAD, SIDE * HEAD)
        ]

    def reach(which, direction):
        return (5 - which % SIDE) if direction == 0 else (2 + which % SIDE)

    def ring_copy(which, direction, s):
        piece = shard(own_slot, which)
        return pltpu.make_async_remote_copy(
            src_ref=piece,
            dst_ref=piece,
            send_sem=z_send.at[direction, s],
            recv_sem=z_recv.at[direction, s],
            device_id=(z_right, z_left)[direction],
            device_id_type=MESH,
        )

    def fan(which):
        source = shard(own_slot, which)
        for k in range(1, SIDE):
            remote(source, source, w_send.at[k - 1], w_recv.at[k - 1], weight_peer(k, core))
        other = shard(pick(core, y, x), which)
        for k in range(SIDE):
            remote(source, other, w_send.at[3 + k], w_recv.at[3 + k], weight_peer(k, 1 - core))

    def ring_wait(s):
        for direction in range(2):
            which = ((z + RING - s - 1) if direction == 0 else (z + s + 1)) % RING

            def arrived(which=which, direction=direction):
                wait_bytes(shard(own_slot, which), z_recv.at[direction, s])
                if s == 0:
                    ring_copy(which, direction, 1).start()
                elif s < 4:
                    pl.when(s + 1 < reach(which, direction))(lambda: ring_copy(which, direction, s + 1).start())
                fan(which)

            if s < 2:
                arrived()
            else:
                pl.when(s < reach(which, direction))(arrived)

    def wait_weights():
        for k in range(1, SIDE):
            wait_bytes(slab((own_slot + SIDE - k) % SIDE, core), w_recv.at[k - 1])
        for k in range(SIDE):
            wait_bytes(slab((own_slot + SIDE - k) % SIDE, 1 - core), w_recv.at[3 + k])

    wait_bytes(shard(own_slot, z), own_sem.at[0])
    for direction in range(2):
        ring_copy(z, direction, 0).start()
    start_kv(0, 0)
    start_kv(0, 1)
    start_q(0)
    fan(z)
    last = len(GROUPS)
    for j in range(PARTS - 1):
        for half in range(2):
            if 2 * j + half < 5:
                ring_wait(2 * j + half)
            wait_kv(j, half)
            if j + 1 < LAST or half == 0:
                start_kv(j + 1, half)
        wait_q(j)
        attend_all(j)
        start_back(j)
        if j + 1 == LAST:
            start_kv(LAST, 1)
        if j + 1 < LAST:
            start_q(j + 1)
        if j >= 1:
            start_tokens(j - 1)
    for copy in residual:
        copy.wait()
    level = timestep[0]
    levels = lax.broadcasted_iota(jnp.int32, gates.shape, 0)
    gate_row = jnp.sum(jnp.where(levels == level, gates[...], 0.0), axis=0, keepdims=True)
    rate_row = jnp.sum(jnp.where(levels == level, rates[...], 0.0), axis=0, keepdims=True)
    gates[0:1, :] = gate_row
    rates[0:1, :] = rate_row

    wait_weights()
    for j in range(2):
        wait_tokens(j)
        project(j)
    wait_kv(LAST, 0)
    start_q(LAST, 0)
    wait_kv(LAST, 1)
    for group in range(1, last):
        start_q(LAST, group)
    start_tokens(3)
    wait_tokens(2)
    project(2)
    for group in range(last):
        wait_q(LAST, group)
        attend(LAST, *GROUPS[group])
        start_back(LAST, group)
    for group in range(last):
        start_tokens(LAST, group)
        if group == 0:
            wait_tokens(3)
            project(3)
    arrived = 0
    for group, (first, count) in enumerate(OUT_GROUPS):
        while arrived < last and GROUPS[arrived][0] < first + count:
            wait_tokens(LAST, arrived)
            arrived += 1
        project_last(group)

    def finish(b, columns, value, value_tan):
        rows = pl.ds(b * UNIT, UNIT)
        gate, rate = gates[0:1, columns], rates[0:1, columns]
        change[0, rows, columns] = gate * value
        change[1, rows, columns] = gate * value_tan + rate * value

    def finish_straight(b):
        for r in range(SIDE):
            for n in range(TILES):
                value = out_recv[b, r, n].astype(jnp.float32)
                finish(b, pl.ds(r * SLICE + n * TILE, TILE), value[0], value[1])

    def finish_crossed(b):
        lower = lax.broadcasted_iota(jnp.int32, (2 * UNIT, HEAD), 1) < HEAD // 2

        def load(r, unit):
            q = unit // 2
            piece = out_recv[b, r, q // 2, :, :, pl.ds((q % 2) * HEAD, HEAD)]
            return piece.astype(jnp.float32).reshape(2 * UNIT, HEAD)

        for t in range(D // HEAD):
            found = []
            for g in (2 * t, 2 * t + 1):
                s, rest = g // 20, g % 20
                found.append((rest // 5, 5 * s + rest % 5))
            (r0, u0), (r1, u1) = found
            first = load(r0, u0)
            if u0 % 2:
                first = pltpu.roll(first, HEAD // 2, 1)
            if r0 == r1 and u0 % 2 == 0 and u1 == u0 + 1:
                value = first
            else:
                second = load(r1, u1)
                if u1 % 2 == 0:
                    second = pltpu.roll(second, HEAD // 2, 1)
                value = jnp.where(lower, first, second)
            finish(b, pl.ds(t * HEAD, HEAD), value[:UNIT], value[UNIT:])

    for group, (first, count) in enumerate(OUT_GROUPS):
        for k in range(1, SIDE):
            wait_bytes(out_recv.at[pl.ds(first, count), (rank + SIDE - k) % SIDE], res_recv.at[group, k - 1])
        for b in range(first, first + count):
            pl.when(core == 0)(lambda b=b: finish_straight(b))
            pl.when(core == 1)(lambda b=b: finish_crossed(b))

    for j in range(PARTS):
        for half in range(2):
            wait_bytes(xkv.at[j, pl.ds(2 * half, 2), pl.ds(0, NT - 1)], kv_send.at[j, half])
        for group in (None,) if j < LAST else range(len(GROUPS)):
            blocks, i = span(group), slot(j, group)
            wait_bytes(xq.at[j, :, blocks, pl.ds(0, NT - 1)], q_send.at[i])
            wait_bytes(att.at[j, blocks, :, pl.ds(0, NT - 1)], back_send.at[i])
            for k in range(SIDE - 1):
                wait_bytes(tok.at[j, rank, blocks], tok_send.at[i, k])
    for direction in range(2):
        for s in range(5):
            which = ((z + RING - s) if direction == 0 else (z + s)) % RING
            done = lambda which=which, direction=direction, s=s: ring_copy(which, direction, s).wait_send()
            if s < 2:
                done()
            else:
                pl.when(s < reach(which, direction))(done)
    for k in range(7):
        wait_bytes(slab(own_slot, core), w_send.at[k])
    for group, (first, count) in enumerate(OUT_GROUPS):
        for k in range(SIDE - 1):
            wait_bytes(out_send.at[pl.ds(first, count), 0], res_send.at[group, k])


def shards(projected, projected_tan, hidden, hidden_tan, out_weight, gate_table, gate_rate, timestep):
    proj = jnp.transpose(projected, (0, 2, 1, 3)).reshape(3, BLOCKS, UNIT, D)
    ptan = jnp.transpose(projected_tan, (0, 2, 1, 3)).reshape(3, BLOCKS, UNIT, D)
    any_spec = pl.BlockSpec(memory_space=pl.ANY)
    vmem = pl.BlockSpec(memory_space=pltpu.VMEM)
    bf16 = jnp.bfloat16
    dma = pltpu.SemaphoreType.DMA
    change = pl.pallas_call(
        kernel,
        out_shape=jax.ShapeDtypeStruct((2, ROWS, D), jnp.float32),
        in_specs=[any_spec] * 5 + [pl.BlockSpec(memory_space=pltpu.SMEM)],
        out_specs=vmem,
        scratch_shapes=[
            pltpu.VMEM((PARTS, 4, NT, BLOCKS, UNIT, HEAD), bf16),
            pltpu.VMEM((PARTS, 2, BLOCKS, NT, UNIT, HEAD), bf16),
            pltpu.VMEM((PARTS, BLOCKS, 2, NT, UNIT, HEAD), bf16),
            pltpu.VMEM((PARTS, SIDE, BLOCKS, 2, UNIT, NT * HEAD), bf16),
            pltpu.VMEM((PARTS, SLICE, NT * HEAD), bf16),
            pltpu.VMEM((TILES, SIDE, BLOCKS, 2 * UNIT, TILE), jnp.float32),
            pltpu.VMEM((BLOCKS, SIDE, TILES, 2, UNIT, TILE), bf16),
            pltpu.VMEM((BLOCKS, SIDE, TILES, 2, UNIT, TILE), bf16),
            pltpu.VMEM((32, D), jnp.float32),
            pltpu.VMEM((32, D), jnp.float32),
            dma((PARTS, 2)),
            dma((PARTS, 2)),
            dma((LAST + len(GROUPS),)),
            dma((LAST + len(GROUPS),)),
            dma((LAST + len(GROUPS),)),
            dma((LAST + len(GROUPS),)),
            dma((LAST + len(GROUPS), SIDE - 1)),
            dma((LAST + len(GROUPS), SIDE - 1)),
            dma((2, 5)),
            dma((2, 5)),
            dma((7,)),
            dma((7,)),
            dma((len(OUT_GROUPS), SIDE - 1)),
            dma((len(OUT_GROUPS), SIDE - 1)),
            dma((2,)),
            dma((1,)),
        ],
        compiler_params=pltpu.CompilerParams(
            collective_id=0, has_side_effects=True, vmem_limit_bytes=56 * 1024 * 1024
        ),
    )(
        proj,
        ptan,
        out_weight.T,
        gate_table,
        gate_rate,
        timestep,
    )
    block_out = (hidden.astype(jnp.float32) + change[:1]).astype(bf16)
    block_tan = (hidden_tan.astype(jnp.float32) + change[1:]).astype(bf16)
    return block_out, block_tan


def solution(mesh):
    return jax.shard_map(
        shards,
        mesh=mesh,
        in_specs=(
            P("dp", "tensor", None, None),
            P("dp", "tensor", None, None),
            P("dp", "tensor", None),
            P("dp", "tensor", None),
            P("tensor", "dp"),
            P(),
            P(),
            P("dp"),
        ),
        out_specs=(P("dp", "tensor", None), P("dp", "tensor", None)),
        check_vma=False,
    )
```
